128 devices in a mesh: clique: 32 (over y, z, core), subtree: 4 (over x).
Axes of the slice: x: 4, y: 4, z: 4, core: 2. Of those that a mesh axis runs over, the one named last changes fastest.
Arguments:
- potentials: float32 [4, 32, 1024, 1024], P('subtree', 'clique'), may hold values from -125 to 125
- parent: int32 [4, 32], P('subtree'), may hold values from 0 to 31, as said below
- child_drop: int32 [4, 32], replicated, may hold values from 0 to 3
- parent_drop: int32 [4, 32], replicated, may hold values from 0 to 3
Outputs:
- log_marginals: float32 [4, 32, 1024, 1024], P('subtree', 'clique')
The draws below stay inside these ranges and needn't reach their ends.
Inputs may be any that keep to these rules, and one draw needn't show every extreme that they name: parent[s, 0] = 0 marks the root of subtree s; every other clique's parent is a clique of the same subtree, and following parents from any clique reaches clique 0 in at most 2 steps.
All inputs are finite; a program needn't handle non-finite values.
Results may differ from the reference program's by a relative error of at most 0.0003.
Values sent between devices are 32-bit elements; how exact they have to be, the bound alone decides.
A program may use at most 192 MiB of HBM per device.

```python
import jax
import jax.numpy as jnp
from jax import lax

LEVELS = 32
DEPTH = 2
CLIQUES = 32
SUBTREES = 4


def one_tree(tree_key):
    first_key, second_key, third_key = jax.random.split(tree_key, 3)
    positions = jnp.arange(CLIQUES, dtype=jnp.int32)
    levels_drawn = jax.random.randint(first_key, (CLIQUES,), 1, DEPTH + 1)
    levels_drawn = jnp.where(positions <= DEPTH, positions, levels_drawn)
    popular = jax.random.randint(second_key, (CLIQUES,), 1, 17)
    popular = popular * popular
    jitter = jax.random.randint(third_key, (CLIQUES, CLIQUES), 0, 1024)
    scores = popular[None, :] * jitter * CLIQUES + positions[None, :]
    allowed = levels_drawn[None, :] == levels_drawn[:, None] - 1
    scores = jnp.where(allowed, scores, -1)
    chosen = jnp.argmax(scores, axis=1).astype(jnp.int32)
    return jnp.where(positions == 0, 0, chosen).astype(jnp.int32)


def draw_parent(key, part):
    subkeys = jax.random.split(jax.random.fold_in(key, 11), SUBTREES)
    return jax.vmap(one_tree)(subkeys)


def draw_potentials(key, part):
    first_key = jax.random.fold_in(jax.random.fold_in(key, 23), 0)
    shape = (SUBTREES, CLIQUES, LEVELS * LEVELS, LEVELS * LEVELS)
    jitter = jax.random.normal(first_key, shape, jnp.float32)
    return 3.0 * jnp.clip(jitter, -5.0, 5.0)


def set_ends(result, own_key, least, largest):
    longest = result.shape.index(max(result.shape))
    spots = []
    for shift in (0, 1):
        where = [jax.random.randint(jax.random.fold_in(own_key, axis), (), 0, length) for axis, length in enumerate(result.shape)]
        where[longest] = (where[longest] + shift) % result.shape[longest]
        spots.append(tuple(where))
    return result.at[spots[0]].set(least).at[spots[1]].set(largest)


def setup_inputs(seed: int = 0) -> dict:
    key_of = jax.random.split(jax.random.key(seed), 5)
    return {
        "potentials": draw_potentials(jax.random.fold_in(key_of[4], 71), 0),
        "parent": draw_parent(jax.random.fold_in(key_of[4], 71), 0),
        "child_drop": set_ends(jax.random.randint(key_of[2], (SUBTREES, CLIQUES), 0, 4), jax.random.fold_in(key_of[2], 1), 0, 3).astype(jnp.int32),
        "parent_drop": set_ends(jax.random.randint(key_of[3], (SUBTREES, CLIQUES), 0, 4), jax.random.fold_in(key_of[3], 1), 0, 3).astype(jnp.int32),
    }


def spread_slots(slot_tables, levels):
    number = slot_tables.shape[0]
    squared = levels * levels
    first = jnp.tile(slot_tables[:, 0].reshape(number, levels, squared), (1, levels, 1))
    second = jnp.repeat(slot_tables[:, 1].reshape(number, levels, squared), levels, axis=1)
    third = jnp.tile(slot_tables[:, 2].reshape(number, squared, levels), (1, 1, levels))
    fourth = jnp.repeat(slot_tables[:, 3].reshape(number, squared, levels), levels, axis=2)
    return first + second + third + fourth


def one_hot_four(dropped):
    return (dropped[:, None] == jnp.arange(4)[None, :]).astype(jnp.float32)


def select_slot(marginal, dropped):
    return jnp.sum(one_hot_four(dropped)[:, :, None] * marginal, axis=1)


def slotted(message, dropped):
    return one_hot_four(dropped)[:, :, None] * message[:, None, :]


def clique_margins(table):
    levels = LEVELS
    hyper = table.reshape(levels, levels, levels, levels)
    parts = [jax.nn.logsumexp(hyper, axis=k).reshape(levels ** 3) for k in range(4)]
    return jnp.stack(parts)


def margins(tables):
    return lax.map(clique_margins, tables)


def reference(potentials, parent, child_drop, parent_drop):
    subtrees, per_subtree = parent.shape
    levels = LEVELS
    squared = levels * levels
    cubed = levels ** 3
    tables = potentials.reshape(subtrees * per_subtree, squared, squared)
    positions = jnp.arange(per_subtree)
    targets = parent * 4 + parent_drop
    slot_index = jnp.arange(4 * per_subtree)
    up_incidence = ((targets[:, None, :] == slot_index[None, :, None]) & (positions != 0)[None, None, :]).astype(jnp.float32)
    down_incidence = (slot_index[None, None, :] == targets[:, :, None]).astype(jnp.float32)
    child_flat = child_drop.reshape(-1)
    parent_flat = parent_drop.reshape(-1)
    incoming = jnp.zeros((subtrees * per_subtree, 4, cubed), jnp.float32)
    for iteration in range(DEPTH):
        upward = tables + spread_slots(incoming, levels)
        message = select_slot(margins(upward), child_flat)
        stacked = message.reshape(subtrees, per_subtree, cubed)
        incoming = jnp.einsum("src,scx->srx", up_incidence, stacked, precision=lax.Precision.HIGHEST).reshape(subtrees * per_subtree, 4, cubed)
    upward = tables + spread_slots(incoming, levels)
    message = select_slot(margins(upward), child_flat)
    root_in = jnp.zeros((1, 4, cubed), jnp.float32)
    root_up = [None] * subtrees
    root_message = [None] * subtrees
    for position in range(subtrees - 1, -1, -1):
        row = position * per_subtree
        root_up[position] = upward[row:row + 1] + spread_slots(root_in, levels)
        root_message[position] = select_slot(margins(root_up[position]), child_flat[row:row + 1])
        root_in = slotted(root_message[position], parent_flat[row:row + 1])
    root_belief = [root_up[0]]
    for position in range(1, subtrees):
        row = position * per_subtree
        correction = select_slot(margins(root_belief[position - 1]), parent_flat[row:row + 1]) - root_message[position]
        root_belief.append(root_up[position] + spread_slots(slotted(correction, child_flat[row:row + 1]), levels))
    roots = jnp.concatenate(root_belief, axis=0)
    belief = upward.reshape(subtrees, per_subtree, squared, squared).at[:, 0].set(roots).reshape(subtrees * per_subtree, squared, squared)
    is_root = (jnp.arange(subtrees * per_subtree) % per_subtree) == 0
    for iteration in range(DEPTH):
        marginal = margins(belief).reshape(subtrees, 4 * per_subtree, cubed)
        received = jnp.einsum("scr,srx->scx", down_incidence, marginal, precision=lax.Precision.HIGHEST).reshape(subtrees * per_subtree, cubed)
        updated = upward + spread_slots(slotted(received - message, child_flat), levels)
        belief = jnp.where(is_root[:, None, None], belief, updated)
    log_total = jax.nn.logsumexp(belief, axis=(1, 2), keepdims=True)
    return (belief - log_total).reshape(subtrees, per_subtree, squared, squared)
```

```python
import functools

import jax
import jax.numpy as jnp
from jax import lax
from jax.experimental import pallas as pl
from jax.experimental.pallas import tpu as pltpu
from jax.sharding import PartitionSpec as P

PIECES = 32
CHUNKS = 8
MESH = pl.DeviceIdType.MESH
F32 = jnp.float32
VMEM = pltpu.VMEM
SMEM = pltpu.SMEM


def lanes():
    return lax.broadcasted_iota(jnp.int32, (8, 128), 1)


def rows():
    return lax.broadcasted_iota(jnp.int32, (8, 128), 0)


def take(vec, index):
    return jnp.take_along_axis(vec, index, axis=1, mode="promise_in_bounds")


def tree(parts, op):
    parts = list(parts)
    while len(parts) > 1:
        parts = [op(*parts[n : n + 2]) if n + 1 < len(parts) else parts[n] for n in range(0, len(parts), 2)]
    return parts[0]


def tile(table, a0, i, t):
    return table[pl.ds(pl.multiple_of(a0 * 32 + 8 * i, 8), 8), 128 * t : 128 * (t + 1)]


def placed(slots, a0, base=None):
    lane, row = lanes(), rows()
    a0_tile, a0_row = a0 // 8, a0 % 8

    def slot_row(k, j):
        return slots[a0_tile * 8 + j, k, pl.ds(a0_row, 1), :]

    second = [slot_row(1, t) for t in range(8)]
    out = []
    for i in range(4):
        both = [jnp.where(row < 4, slot_row(k, 2 * i), slot_row(k, 2 * i + 1)) for k in (2, 3)]
        third = take(both[0], (row % 4) * 32 + lane % 32)
        out.append(
            [
                (slots[i * 8 + t, 0] + second[t])
                + (third + take(both[1], (row % 4) * 32 + lane // 32 + 4 * t))
                for t in range(8)
            ]
        )
    return out


def margin_0(table, store):
    def body(i, carry):
        for t in range(8):
            parts = [tile(table, a0, i, t) for a0 in range(32)]
            top = tree(parts, jnp.maximum)
            total = tree([jnp.exp(part - top) for part in parts], jnp.add)
            store(i * 8 + t, None, top + jnp.log(total))
        return carry

    lax.fori_loop(0, 4, body, 0)


def margin_1(table, store):
    def over_rows(vec, op):
        for shift in (4, 2, 1):
            vec = op(vec, pltpu.roll(vec, shift, 0))
        return vec

    def body(a0, carry):
        for t in range(8):
            parts = [tile(table, a0, i, t) for i in range(4)]
            top = over_rows(tree(parts, jnp.maximum), jnp.maximum)
            total = over_rows(tree([jnp.exp(part - top) for part in parts], jnp.add), jnp.add)
            store((a0 // 8) * 8 + t, a0 % 8, (top + jnp.log(total))[0:1])
        return carry

    lax.fori_loop(0, 32, body, 0)


def store_packed(result, a0, i, store):
    packed = jnp.where(lanes() // 32 == rows() % 4, result, 0.0)
    packed = packed + pltpu.roll(packed, 1, 0)
    packed = packed + pltpu.roll(packed, 2, 0)
    store((a0 // 8) * 8 + 2 * i, a0 % 8, packed[3:4])
    store((a0 // 8) * 8 + 2 * i + 1, a0 % 8, packed[7:8])


def margin_2(table, store):
    def over_groups(vec, op):
        for shift in (64, 32):
            vec = op(vec, pltpu.roll(vec, shift, 1))
        return vec

    def body(a0, carry):
        for i in range(4):
            parts = [tile(table, a0, i, t) for t in range(8)]
            top = over_groups(tree(parts, jnp.maximum), jnp.maximum)
            total = over_groups(tree([jnp.exp(part - top) for part in parts], jnp.add), jnp.add)
            store_packed(top + jnp.log(total), a0, i, store)
        return carry

    lax.fori_loop(0, 32, body, 0)


def margin_3(table, store):
    lane = lanes()

    def over_lanes(parts, op):
        parts = list(parts)
        for shift in (16, 8, 4):
            upper = (lane & shift) != 0
            half = len(parts) // 2
            parts = [
                op(
                    jnp.where(upper, high, low),
                    take(jnp.where(upper, low, high), lane ^ shift),
                )
                for low, high in zip(parts[:half], parts[half:])
            ]
        vec = parts[0]
        for shift in (2, 1):
            vec = op(vec, take(vec, lane ^ shift))
        return vec

    def body(a0, carry):
        for i in range(4):
            parts = [tile(table, a0, i, t) for t in range(8)]
            top = over_lanes(parts, jnp.maximum)
            total = over_lanes(
                [jnp.exp(part - take(top, (lane // 32) * 32 + 4 * t)) for t, part in enumerate(parts)],
                jnp.add,
            )
            level = lane % 32
            result = take(top + jnp.log(total), (level % 4) * 32 + (level // 4) * 4)
            store_packed(result, a0, i, store)
        return carry

    lax.fori_loop(0, 32, body, 0)


MARGINS = (margin_0, margin_1, margin_2, margin_3)


def message_store(message):
    def store(piece, row, value):
        if row is None:
            message[piece] = value
        else:
            message[piece, pl.ds(row, 1), :] = value

    return store


def slot_store(slots, k):
    def store(piece, row, value):
        if row is None:
            slots[piece, k] = value
        else:
            slots[piece, k, pl.ds(row, 1), :] = value

    return store


def chosen_margin(table, axis, message):
    for k in range(4):

        @pl.when(axis == k)
        def _(k=k):
            MARGINS[k](table, message_store(message))


def chunk_copy(source, table, sems, chunk):
    size = 1024 // CHUNKS
    part = pl.ds(pl.multiple_of(chunk * size, size), size)
    return pltpu.make_async_copy(source.at[part], table.at[part], sems.at[chunk])


def load(potentials, table, sems):
    for chunk in range(CHUNKS):
        chunk_copy(potentials, table, sems, chunk).start()


def wait_load(potentials, table, sems):
    for chunk in range(CHUNKS):
        chunk_copy(potentials, table, sems, chunk).wait()


def place_all(potentials, table, sems, slots, after=None):
    per_chunk = 32 // CHUNKS

    def chunk_body(chunk, carry):
        chunk_copy(potentials, table, sems, chunk).wait()

        def body(n, inner):
            a0 = chunk * per_chunk + n
            add = placed(slots, a0)
            for i in range(4):
                for t in range(8):
                    where = pl.ds(pl.multiple_of(a0 * 32 + 8 * i, 8), 8)
                    table[where, 128 * t : 128 * (t + 1)] = tile(table, a0, i, t) + add[i][t]
            return inner

        lax.fori_loop(0, per_chunk, body, 0)
        if after is not None:
            after(chunk)
        return carry

    lax.fori_loop(0, CHUNKS, chunk_body, 0)


def add_slot(slots, k, message, minus=None, shift=None):
    def body(piece, carry):
        value = message[piece]
        if minus is not None:
            value = value - minus[piece]
        if shift is not None:
            value = value - shift
        slots[piece, k] = slots[piece, k] + value
        return carry

    lax.fori_loop(0, PIECES, body, 0)


def copy_slots(source, target):
    def body(piece, carry):
        for k in range(4):
            target[piece, k] = source[piece, k]
        return carry

    lax.fori_loop(0, PIECES, body, 0)


def first_kernel(parent, child_drop, parent_drop, potentials, message, previous, last, table, sems):
    me, tree_here = lax.axis_index("clique"), lax.axis_index("subtree")
    load(potentials, table, sems)

    def clear(n, carry):
        last[n] = PIECES
        return carry

    lax.fori_loop(0, 128, clear, 0)
    previous[0] = PIECES

    def link(c, carry):
        target = parent[0, c] * 4 + parent_drop[tree_here, c]
        previous[c] = last[target]
        last[target] = c
        return carry

    lax.fori_loop(1, PIECES, link, 0)
    wait_load(potentials, table, sems)
    chosen_margin(table, child_drop[tree_here, me], message)


def up_kernel(child_drop, potentials, slots, message, table, sems):
    me, tree_here = lax.axis_index("clique"), lax.axis_index("subtree")
    load(potentials, table, sems)
    place_all(potentials, table, sems, slots)
    chosen_margin(table, child_drop[tree_here, me], message)


def chain_slot(step, s, child_drop, parent_drop):
    from_next = parent_drop[jnp.minimum(s + 1, 3), 0]
    from_previous = child_drop[s, 0]
    if step == 1:
        return jnp.where(s == 2, from_next, from_previous)
    if step == 2:
        return jnp.where(s == 1, from_next, from_previous)
    return jnp.where(s == 0, from_next, from_previous)


def chain_kernel(step, *refs):
    child_drop, parent_drop, potentials, slots = refs[:4]
    message, table, held, sems = refs[-4:]
    s = lax.axis_index("subtree")
    load(potentials, table, sems)
    to_next = parent_drop[jnp.minimum(s + 1, 3), 0]
    to_previous = child_drop[s, 0]
    axis = jnp.where(s == {1: 0, 2: 1, 3: 2}[step], to_next, to_previous)
    if step == 1:
        place_all(potentials, table, sems, slots)
    else:
        copy_slots(slots, held)
        add_slot(held, chain_slot(step - 1, s, child_drop, parent_drop), refs[4])
        place_all(potentials, table, sems, held)
    chosen_margin(table, axis, message)


def root_margins_kernel(child_drop, parent_drop, potentials, slots, first, second, third, margins, full, table, sems):
    me, s = lax.axis_index("clique"), lax.axis_index("subtree")
    load(potentials, table, sems)
    copy_slots(slots, full)

    @pl.when(me == 0)
    def _():
        for step, arrived in ((1, first), (2, second), (3, third)):
            add_slot(full, chain_slot(step, s, child_drop, parent_drop), arrived)

    place_all(potentials, table, sems, full)
    for k in range(4):
        MARGINS[k](table, slot_store(margins, k))


def child_margins_kernel(child_drop, potentials, slots, received, message, margins, table, held, sems):
    me, s = lax.axis_index("clique"), lax.axis_index("subtree")
    load(potentials, table, sems)
    copy_slots(slots, held)

    @pl.when(me != 0)
    def _():
        add_slot(held, child_drop[s, me], received, minus=message)

    place_all(potentials, table, sems, held)
    for k in range(4):
        MARGINS[k](table, slot_store(margins, k))


def final_kernel(child_drop, potentials, slots, received, message, out, table, held, sems, out_sems):
    me, s = lax.axis_index("clique"), lax.axis_index("subtree")
    load(potentials, table, sems)
    copy_slots(slots, held)
    top = received[0]
    for piece in range(1, PIECES):
        top = jnp.maximum(top, received[piece])
    top = jnp.max(top)
    total = jnp.zeros((8, 128), F32)
    for piece in range(PIECES):
        total = total + jnp.exp(received[piece] - top)
    log_total = top + jnp.log(jnp.broadcast_to(jnp.sum(total), (8, 128)))
    drop = child_drop[s, me]

    @pl.when(me != 0)
    def _():
        add_slot(held, drop, received, minus=message, shift=log_total)

    @pl.when(me == 0)
    def _():
        def body(piece, carry):
            held[piece, drop] = held[piece, drop] - log_total
            return carry

        lax.fori_loop(0, PIECES, body, 0)

    size = 1024 // CHUNKS

    def out_copy(chunk):
        part = pl.ds(pl.multiple_of(chunk * size, size), size)
        return pltpu.make_async_copy(table.at[part], out.at[part], out_sems.at[chunk])

    place_all(potentials, table, sems, held, after=lambda chunk: out_copy(chunk).start())
    for chunk in range(CHUNKS):
        out_copy(chunk).wait()


def enter(me):
    barrier = pltpu.get_barrier_semaphore()

    def body(d, carry):
        pl.semaphore_signal(barrier, inc=1, device_id={"clique": (me + d) % PIECES}, device_id_type=MESH)
        return carry

    lax.fori_loop(1, PIECES, body, 0)
    pl.semaphore_wait(barrier, PIECES - 1)


def send_pieces(me, source, target, sems):
    def body(d, carry):
        other = (me + d) % PIECES
        pltpu.make_async_remote_copy(
            src_ref=source.at[other],
            dst_ref=target.at[me],
            send_sem=sems.at[0],
            recv_sem=sems.at[1],
            device_id={"clique": other},
            device_id_type=MESH,
        ).start()
        return carry

    lax.fori_loop(1, PIECES, body, 0)


def all_but_one(me, source, target, sems):
    return pltpu.make_async_remote_copy(
        src_ref=source.at[pl.ds(0, PIECES - 1)],
        dst_ref=target.at[pl.ds(0, PIECES - 1)],
        send_sem=sems.at[0],
        recv_sem=sems.at[1],
        device_id={"clique": (me + 1) % PIECES},
        device_id_type=MESH,
    )


def gather_up(me, previous, last, message, arrived, sums, sems):
    enter(me)
    send_pieces(me, message, arrived, sems)
    arrived[me] = message[me]
    all_but_one(me, message, arrived, sems).wait_recv()
    sums[PIECES] = jnp.zeros((8, 128), F32)
    for c in range(1, PIECES):
        sums[c] = arrived[c] + sums[previous[c]]
    all_but_one(me, message, arrived, sems).wait_send()


def sums_kernel(previous, last, message, slots, arrived, sums, outgoing, incoming, sems, more_sems):
    me = lax.axis_index("clique")
    gather_up(me, previous, last, message, arrived, sums, sems)

    def body(p, carry):
        for k in range(4):
            outgoing[p, k] = sums[last[p * 4 + k]]
        return carry

    lax.fori_loop(0, PIECES, body, 0)
    send_pieces(me, outgoing, incoming, more_sems)
    incoming[me] = outgoing[me]
    all_but_one(me, outgoing, incoming, more_sems).wait()
    copy_slots(incoming, slots)


def root_sums_kernel(previous, last, message, old_slots, slots, arrived, sums, outgoing, incoming, sems, more_sems):
    me = lax.axis_index("clique")
    gather_up(me, previous, last, message, arrived, sums, sems)
    for k in range(4):
        outgoing[k] = sums[last[k]]

    @pl.when(me != 0)
    def _():
        copy = pltpu.make_async_remote_copy(
            src_ref=outgoing,
            dst_ref=incoming.at[me],
            send_sem=more_sems.at[0],
            recv_sem=more_sems.at[1],
            device_id={"clique": 0},
            device_id_type=MESH,
        )
        copy.start()
        copy_slots(old_slots, slots)
        copy.wait_send()

    @pl.when(me == 0)
    def _():
        for k in range(4):
            slots[0, k] = outgoing[k]
        pltpu.make_async_remote_copy(
            src_ref=incoming.at[pl.ds(1, PIECES - 1)],
            dst_ref=incoming.at[pl.ds(1, PIECES - 1)],
            send_sem=more_sems.at[0],
            recv_sem=more_sems.at[1],
            device_id={"clique": 1},
            device_id_type=MESH,
        ).wait_recv()

        def body(piece, carry):
            for k in range(4):
                slots[piece, k] = incoming[piece, k]
            return carry

        lax.fori_loop(1, PIECES, body, 0)


def send_received(me, outgoing, received, incoming, sems):
    send_pieces(me, outgoing, incoming, sems)
    incoming[me] = outgoing[me]
    all_but_one(me, outgoing, incoming, sems).wait()

    def body(piece, carry):
        received[piece] = incoming[piece]
        return carry

    lax.fori_loop(0, PIECES, body, 0)


def root_spread_kernel(parent_drop, margins, received, arrived, outgoing, incoming, sems, more_sems):
    me, s = lax.axis_index("clique"), lax.axis_index("subtree")
    enter(me)

    @pl.when(me == 0)
    def _():
        def body(other, carry):
            pltpu.make_async_remote_copy(
                src_ref=margins.at[other],
                dst_ref=arrived,
                send_sem=sems.at[0],
                recv_sem=sems.at[1],
                device_id={"clique": other},
                device_id_type=MESH,
            ).start()
            return carry

        lax.fori_loop(1, PIECES, body, 0)
        for k in range(4):
            arrived[k] = margins[0, k]

    @pl.when(me != 0)
    def _():
        pltpu.make_async_remote_copy(
            src_ref=arrived,
            dst_ref=arrived,
            send_sem=sems.at[0],
            recv_sem=sems.at[1],
            device_id={"clique": 0},
            device_id_type=MESH,
        ).wait_recv()

    for c in range(PIECES):
        outgoing[c] = arrived[parent_drop[s, c]]
    send_received(me, outgoing, received, incoming, more_sems)

    @pl.when(me == 0)
    def _():
        pltpu.make_async_remote_copy(
            src_ref=margins.at[pl.ds(1, PIECES - 1)],
            dst_ref=margins.at[pl.ds(1, PIECES - 1)],
            send_sem=sems.at[0],
            recv_sem=sems.at[1],
            device_id={"clique": 1},
            device_id_type=MESH,
        ).wait_send()


def spread_kernel(parent, parent_drop, margins, received, arrived, outgoing, incoming, sems, more_sems):
    me, s = lax.axis_index("clique"), lax.axis_index("subtree")
    enter(me)
    send_pieces(me, margins, arrived, sems)
    arrived[me] = margins[me]
    all_but_one(me, margins, arrived, sems).wait_recv()
    for c in range(PIECES):
        outgoing[c] = arrived[parent[0, c], parent_drop[s, c]]
    send_received(me, outgoing, received, incoming, more_sems)
    all_but_one(me, margins, arrived, sems).wait_send()


MESSAGE = jax.ShapeDtypeStruct((PIECES, 8, 128), F32)
SLOTS = jax.ShapeDtypeStruct((PIECES, 4, 8, 128), F32)
TABLE = jax.ShapeDtypeStruct((1024, 1024), F32)
ANY_SPEC = pl.BlockSpec(memory_space=pl.ANY)
S_SPEC = pl.BlockSpec(memory_space=SMEM)
V_SPEC = pl.BlockSpec(memory_space=VMEM)
HELD_MESSAGE = VMEM((PIECES, 8, 128), F32)
HELD_SUMS = VMEM((PIECES + 1, 8, 128), F32)
HELD_SLOTS = VMEM((PIECES, 4, 8, 128), F32)
HELD_PIECE = VMEM((4, 8, 128), F32)
HELD_TABLE = VMEM((1024, 1024), F32)
LOAD_SEMS = pltpu.SemaphoreType.DMA((CHUNKS,))
PAIR_SEMS = pltpu.SemaphoreType.DMA((2,))


def call(kernel, name, ins, outs, out_specs, scratch, collective=None):
    more = {} if collective is None else dict(collective_id=collective, has_side_effects=True)
    return pl.pallas_call(
        kernel,
        name=name,
        in_specs=ins,
        out_shape=outs,
        out_specs=out_specs,
        scratch_shapes=scratch,
        compiler_params=pltpu.CompilerParams(vmem_limit_bytes=40 * 2**20, **more),
    )


def per_device(potentials, parent, child_drop, parent_drop):
    table = potentials.reshape(1024, 1024)
    compute = [HELD_TABLE]
    message, previous, last = call(
        first_kernel,
        "first",
        [S_SPEC] * 3 + [ANY_SPEC],
        (MESSAGE, jax.ShapeDtypeStruct((PIECES,), jnp.int32), jax.ShapeDtypeStruct((4 * PIECES,), jnp.int32)),
        (V_SPEC, S_SPEC, S_SPEC),
        [HELD_TABLE, LOAD_SEMS],
    )(parent, child_drop, parent_drop, table)
    slots = call(
        sums_kernel,
        "sums",
        [S_SPEC] * 2 + [V_SPEC],
        SLOTS,
        V_SPEC,
        [HELD_MESSAGE, HELD_SUMS, HELD_SLOTS, HELD_SLOTS, PAIR_SEMS, PAIR_SEMS],
        collective=0,
    )(previous, last, message)
    message = call(
        up_kernel, "up", [S_SPEC, ANY_SPEC, V_SPEC], MESSAGE, V_SPEC, [HELD_TABLE, LOAD_SEMS]
    )(child_drop, table, slots)
    slots = call(
        root_sums_kernel,
        "root_sums",
        [S_SPEC] * 2 + [V_SPEC] * 2,
        SLOTS,
        V_SPEC,
        [HELD_MESSAGE, HELD_SUMS, HELD_PIECE, HELD_SLOTS, PAIR_SEMS, PAIR_SEMS],
        collective=1,
    )(previous, last, message, slots)
    arrived = []
    for step, pairs in ((1, ((3, 2), (0, 1))), (2, ((2, 1), (1, 2))), (3, ((1, 0), (2, 3)))):
        sent = call(
            functools.partial(chain_kernel, step),
            f"chain_{step}",
            [S_SPEC] * 2 + [ANY_SPEC] + [V_SPEC] * (1 if step == 1 else 2),
            MESSAGE,
            V_SPEC,
            [HELD_TABLE, HELD_SLOTS, LOAD_SEMS],
        )(child_drop, parent_drop, table, slots, *arrived[step - 2 : step - 1])
        arrived.append(lax.ppermute(sent, ("clique", "subtree"), pairs))
    margins, slots = call(
        root_margins_kernel,
        "root_margins",
        [S_SPEC] * 2 + [ANY_SPEC] + [V_SPEC] * 4,
        (SLOTS, SLOTS),
        (V_SPEC, V_SPEC),
        [HELD_TABLE, LOAD_SEMS],
    )(child_drop, parent_drop, table, slots, *arrived)
    received = call(
        root_spread_kernel,
        "root_spread",
        [S_SPEC, V_SPEC],
        MESSAGE,
        V_SPEC,
        [HELD_PIECE, HELD_MESSAGE, HELD_MESSAGE, PAIR_SEMS, PAIR_SEMS],
        collective=2,
    )(parent_drop, margins)
    margins = call(
        child_margins_kernel,
        "child_margins",
        [S_SPEC, ANY_SPEC] + [V_SPEC] * 3,
        SLOTS,
        V_SPEC,
        [HELD_TABLE, HELD_SLOTS, LOAD_SEMS],
    )(child_drop, table, slots, received, message)
    received = call(
        spread_kernel,
        "spread",
        [S_SPEC, S_SPEC, V_SPEC],
        MESSAGE,
        V_SPEC,
        [HELD_SLOTS, HELD_MESSAGE, HELD_MESSAGE, PAIR_SEMS, PAIR_SEMS],
        collective=3,
    )(parent, parent_drop, margins)
    out = call(
        final_kernel,
        "final",
        [S_SPEC, ANY_SPEC] + [V_SPEC] * 3,
        TABLE,
        ANY_SPEC,
        [HELD_TABLE, HELD_SLOTS, LOAD_SEMS, LOAD_SEMS],
    )(child_drop, table, slots, received, message)
    return out.reshape(1, 1, 1024, 1024)


def solution(mesh):
    specs = (P("subtree", "clique", None, None), P("subtree", None), P(), P())
    return jax.shard_map(
        per_device,
        mesh=mesh,
        in_specs=specs,
        out_specs=P("subtree", "clique", None, None),
        check_vma=False,
    )
```

```python
import functools

import jax
import jax.numpy as jnp
from jax import lax
from jax.experimental import pallas as pl
from jax.experimental.pallas import tpu as pltpu
from jax.sharding import PartitionSpec as P

PIECES = 32
CHUNKS = 8
MESH = pl.DeviceIdType.MESH
F32 = jnp.float32
VMEM = pltpu.VMEM
SMEM = pltpu.SMEM


def lanes():
    return lax.broadcasted_iota(jnp.int32, (8, 128), 1)


def rows():
    return lax.broadcasted_iota(jnp.int32, (8, 128), 0)


def take(vec, index):
    return jnp.take_along_axis(vec, index, axis=1, mode="promise_in_bounds")


def tree(parts, op):
    parts = list(parts)
    while len(parts) > 1:
        parts = [op(*parts[n : n + 2]) if n + 1 < len(parts) else parts[n] for n in range(0, len(parts), 2)]
    return parts[0]


def tile(table, a0, i, t):
    return table[pl.ds(pl.multiple_of(a0 * 32 + 8 * i, 8), 8), 128 * t : 128 * (t + 1)]


def place(source, target, terms, after=None):
    lane, row = lanes(), rows()
    spread_third = (row % 4) * 32 + lane % 32
    spread_fourth = [(row % 4) * 32 + lane // 32 + 4 * t for t in range(8)]

    def body(part, carry):
        for s in range(8):
            a0 = part * 8 + s

            def slot_row(k, j):
                return terms[k][1](part * 8 + j, s)

            second = [slot_row(1, t) for t in range(8)] if 1 in terms else None
            for i in range(4):
                both = {
                    k: jnp.where(row < 4, slot_row(k, 2 * i), slot_row(k, 2 * i + 1))
                    for k in (2, 3)
                    if k in terms
                }
                third = take(both[2], spread_third) if 2 in terms else None
                for t in range(8):
                    adds = [tile(source, a0, i, t)]
                    if 0 in terms:
                        adds.append(terms[0][0](i * 8 + t))
                    if 1 in terms:
                        adds.append(jnp.broadcast_to(second[t], (8, 128)))
                    if 2 in terms:
                        adds.append(third)
                    if 3 in terms:
                        adds.append(take(both[3], spread_fourth[t]))
                    where = pl.ds(pl.multiple_of(a0 * 32 + 8 * i, 8), 8)
                    target[where, 128 * t : 128 * (t + 1)] = tree(adds, jnp.add)
        if after is not None:
            after(part)
        return carry

    lax.fori_loop(0, 4, body, 0)


def place_slots(source, target, slots, after=None):
    def readers(k):
        return lambda piece: slots[piece, k], lambda piece, s: slots[piece, k, pl.ds(s, 1), :]

    place(source, target, {k: readers(k) for k in range(4)}, after)


def place_message(source, target, message, axis, after=None):
    for k in range(4):

        @pl.when(axis == k)
        def _(k=k):
            readers = (lambda piece: message[piece], lambda piece, s: message[piece, pl.ds(s, 1), :])
            place(source, target, {k: readers}, after)


def pick(parts):
    group = lanes() // 32
    return jnp.where(
        group == 0, parts[0], jnp.where(group == 1, parts[1], jnp.where(group == 2, parts[2], parts[3]))
    )


def margin_0(table, put, work):
    def body(i, carry):
        for t in range(8):
            parts = [tile(table, a0, i, t) for a0 in range(32)]
            top = tree(parts, jnp.maximum)
            total = tree([jnp.exp(part - top) for part in parts], jnp.add)
            put(i * 8 + t, 1, None, top + jnp.log(total))
        return carry

    lax.fori_loop(0, 4, body, 0)


def over_rows(vec, op):
    for shift in (4, 2, 1):
        vec = op(vec, pltpu.roll(vec, shift, 0))
    return vec


def margin_1(table, put, work):
    def body(a0, carry):
        for t in range(8):
            parts = [tile(table, a0, i, t) for i in range(4)]
            top = over_rows(tree(parts, jnp.maximum), jnp.maximum)
            total = over_rows(tree([jnp.exp(part - top) for part in parts], jnp.add), jnp.add)
            put((a0 // 8) * 8 + t, 1, a0 % 8, (top + jnp.log(total))[0:1])
        return carry

    lax.fori_loop(0, 32, body, 0)


def margin_2(table, put, work):
    totals, tops = work[0], work[1]

    def largest(a0, carry):
        for i in range(4):
            at = pl.ds(pl.multiple_of((a0 * 4 + i) * 8, 8), 8)
            totals[at, :] = tree([tile(table, a0, i, t) for t in range(8)], jnp.maximum)
        return carry

    lax.fori_loop(0, 32, largest, 0, unroll=4)

    def groups(n, carry):
        ats = [pl.ds(pl.multiple_of((n * 32 + m) * 8, 8), 8) for m in range(32)]
        parts = [totals[at, :] for at in ats]
        for shift in (64, 32):
            moved = [pltpu.roll(part, shift, 1) for part in parts]
            parts = [jnp.maximum(part, other) for part, other in zip(parts, moved)]
        for at, part in zip(ats, parts):
            tops[at, :] = part
        return carry

    lax.fori_loop(0, 4, groups, 0)

    def sums(a0, carry):
        for i in range(4):
            at = pl.ds(pl.multiple_of((a0 * 4 + i) * 8, 8), 8)
            top = tops[at, :]
            totals[at, :] = tree([jnp.exp(tile(table, a0, i, t) - top) for t in range(8)], jnp.add)
        return carry

    lax.fori_loop(0, 32, sums, 0, unroll=2)

    def pack(part, carry):
        packed = []
        for s in range(8):
            start = (part * 8 + s) * 32
            total = [totals[pl.ds(start + q, 8, stride=4), :] for q in range(4)]
            top = pick([tops[pl.ds(start + q, 8, stride=4), :] for q in range(4)])
            turned = [pick([total[(g + r) % 4] for g in range(4)]) for r in range(4)]
            packed.append((top, [turned[0]] + [pltpu.roll(turned[r], 32 * r, 1) for r in range(1, 4)]))
        for s, (top, turned) in enumerate(packed):
            put(part * 8, 8, s, top + jnp.log((turned[0] + turned[1]) + (turned[2] + turned[3])))
        return carry

    lax.fori_loop(0, 4, pack, 0)


def margin_3(table, put, work):
    flat, across = work[0], work[2]

    def body(block, carry):
        for t in range(8):
            turned = table[pl.ds(pl.multiple_of(block * 128, 128), 128), 128 * t : 128 * (t + 1)].T
            for g in range(4):
                parts = [turned[32 * g + 8 * m : 32 * g + 8 * (m + 1)] for m in range(4)]
                top = over_rows(tree(parts, jnp.maximum), jnp.maximum)
                total = over_rows(tree([jnp.exp(part - top) for part in parts], jnp.add), jnp.add)
                across[block, 4 * t + g : 4 * t + g + 1, :] = (top + jnp.log(total))[0:1]
        return carry

    lax.fori_loop(0, 8, body, 0, unroll=2)
    for block in range(8):
        part = across[block]
        flat[128 * block : 128 * (block + 1), :] = jnp.concatenate([part] * 4, axis=0).T
    for a0 in range(32):
        put((a0 // 8) * 8, 8, a0 % 8, pick([flat[pl.ds(a0 * 32 + q, 8, stride=4), :] for q in range(4)]))


MARGINS = (margin_0, margin_1, margin_2, margin_3)


def message_put(message):
    def put(piece, count, row, value):
        if row is None:
            message[piece] = value
        elif count == 1:
            message[piece, pl.ds(row, 1), :] = value
        else:
            message[pl.ds(piece, count), row, :] = value

    return put


def slot_put(slots, k):
    def put(piece, count, row, value):
        if row is None:
            slots[piece, k] = value
        elif count == 1:
            slots[piece, k, pl.ds(row, 1), :] = value
        else:
            slots[pl.ds(piece, count), k, row, :] = value

    return put


def chosen_margin(table, axis, message, work):
    for k in range(4):

        @pl.when(axis == k)
        def _(k=k):
            MARGINS[k](table, message_put(message), work)


def copy_slots(source, target):
    def body(piece, carry):
        for k in range(4):
            target[piece, k] = source[piece, k]
        return carry

    lax.fori_loop(0, PIECES, body, 0)


PREVIOUS, LAST, SOURCE, OWN_DROP, CHAIN_AXIS, CHAIN_SLOT, INFO = 0, 32, 160, 192, 192, 196, 256


def first_kernel(trees_in, potentials, message, info, table, trees, *rest):
    work, load_sems, sems = rest[:3], rest[3], rest[4]
    me, s = lax.axis_index("clique"), lax.axis_index("subtree")
    size = 1024 // CHUNKS
    loads = [
        pltpu.make_async_copy(
            potentials.at[pl.ds(size * n, size)], table.at[pl.ds(size * n, size)], load_sems.at[n]
        )
        for n in range(CHUNKS)
    ]
    small = pltpu.make_async_copy(trees_in, trees, sems)
    small.start()
    for copy in loads:
        copy.start()
    for n in range(128):
        info[LAST + n] = PIECES
    small.wait()
    info[PREVIOUS] = PIECES
    info[SOURCE] = trees[4 + s, 0]

    def link(c, carry):
        target = trees[8, c] * 4 + trees[4 + s, c]
        info[SOURCE + c] = target
        info[PREVIOUS + c] = info[LAST + target]
        info[LAST + target] = c
        return carry

    lax.fori_loop(1, PIECES, link, 0)
    own = trees[s, me]
    info[OWN_DROP] = own
    to_next = trees[4 + jnp.minimum(s + 1, 3), 0]
    to_previous = trees[s, 0]
    for step, sender, receiver in ((1, 0, 2), (2, 1, 1), (3, 2, 0)):
        info[CHAIN_AXIS + step] = jnp.where(s == sender, to_next, to_previous)
        info[CHAIN_SLOT + step] = jnp.where(s == receiver, to_next, to_previous)
    for copy in loads:
        copy.wait()
    chosen_margin(table, own, message, work)


def up_kernel(info, table, slots, message, placed, *work):
    place_slots(table, placed, slots)
    chosen_margin(placed, info[OWN_DROP], message, work)


def chain_first_kernel(info, table, slots, message, placed, *work):
    place_slots(table, placed, slots)
    chosen_margin(placed, info[CHAIN_AXIS + 1], message, work)


def chain_kernel(step, info, table, arrived, message, placed, *work):
    place_message(table, placed, arrived, info[CHAIN_SLOT + step - 1])
    chosen_margin(placed, info[CHAIN_AXIS + step], message, work)


def all_margins(table, margins, work):
    for k in range(4):
        MARGINS[k](table, slot_put(margins, k), work)


def root_margins_kernel(info, table, first, third, margins, belief, held, *work):
    s = lax.axis_index("subtree")
    inner = (s == 1) | (s == 2)

    def body(piece, carry):
        held[piece] = jnp.where(inner, first[piece], third[piece])
        return carry

    lax.fori_loop(0, PIECES, body, 0)
    place_message(table, belief, held, jnp.where(inner, info[CHAIN_SLOT + 1], info[CHAIN_SLOT + 3]))
    all_margins(belief, margins, work)


def child_margins_kernel(info, table, received, message, margins, belief, held, *work):
    below = lax.axis_index("clique") != 0

    def body(piece, carry):
        held[piece] = jnp.where(below, received[piece] - message[piece], 0.0)
        return carry

    lax.fori_loop(0, PIECES, body, 0)
    place_message(table, belief, held, info[OWN_DROP])
    all_margins(belief, margins, work)


def final_kernel(info, table, received, message, out, belief, held, sems):
    below = lax.axis_index("clique") != 0
    top = jnp.max(tree([received[piece] for piece in range(PIECES)], jnp.maximum))
    total = tree([jnp.exp(received[piece] - top) for piece in range(PIECES)], jnp.add)
    log_total = top + jnp.log(jnp.broadcast_to(jnp.sum(total), (8, 128)))
    for piece in range(PIECES):
        held[piece] = jnp.where(below, received[piece] - message[piece], 0.0) - log_total

    def out_copy(part):
        at = pl.ds(pl.multiple_of(part * 256, 256), 256)
        return pltpu.make_async_copy(belief.at[at], out.at[at], sems.at[part])

    place_message(table, belief, held, info[OWN_DROP], after=lambda part: out_copy(part).start())
    for part in range(4):
        out_copy(part).wait()


def enter(me):
    barrier = pltpu.get_barrier_semaphore()

    def body(d, carry):
        pl.semaphore_signal(barrier, inc=1, device_id={"clique": (me + d) % PIECES}, device_id_type=MESH)
        return carry

    lax.fori_loop(1, PIECES, body, 0)
    pl.semaphore_wait(barrier, PIECES - 1)


def send_pieces(me, source, target, sems):
    def body(d, carry):
        other = (me + d) % PIECES
        pltpu.make_async_remote_copy(
            src_ref=source.at[other],
            dst_ref=target.at[me],
            send_sem=sems.at[0],
            recv_sem=sems.at[1],
            device_id={"clique": other},
            device_id_type=MESH,
        ).start()
        return carry

    lax.fori_loop(1, PIECES, body, 0)


def all_but_one(me, source, target, sems):
    return pltpu.make_async_remote_copy(
        src_ref=source.at[pl.ds(0, PIECES - 1)],
        dst_ref=target.at[pl.ds(0, PIECES - 1)],
        send_sem=sems.at[0],
        recv_sem=sems.at[1],
        device_id={"clique": (me + 1) % PIECES},
        device_id_type=MESH,
    )


def gather_up(me, info, message, arrived, sums, sems):
    enter(me)
    send_pieces(me, message, arrived, sems)
    arrived[me] = message[me]
    all_but_one(me, message, arrived, sems).wait_recv()
    sums[PIECES] = jnp.zeros((8, 128), F32)
    for c in range(1, PIECES):
        sums[c] = arrived[c] + sums[info[PREVIOUS + c]]
    all_but_one(me, message, arrived, sems).wait_send()


def sums_kernel(info, message, slots, arrived, sums, outgoing, incoming, sems, more_sems):
    me = lax.axis_index("clique")
    gather_up(me, info, message, arrived, sums, sems)

    def body(p, carry):
        for k in range(4):
            outgoing[p, k] = sums[info[LAST + p * 4 + k]]
        return carry

    lax.fori_loop(0, PIECES, body, 0)
    send_pieces(me, outgoing, incoming, more_sems)
    incoming[me] = outgoing[me]
    all_but_one(me, outgoing, incoming, more_sems).wait()
    copy_slots(incoming, slots)


def root_sums_kernel(info, message, old_slots, slots, arrived, sums, outgoing, incoming, sems, more_sems):
    me = lax.axis_index("clique")
    gather_up(me, info, message, arrived, sums, sems)
    for k in range(4):
        outgoing[k] = sums[info[LAST + k]]

    @pl.when(me != 0)
    def _():
        copy = pltpu.make_async_remote_copy(
            src_ref=outgoing,
            dst_ref=incoming.at[me],
            send_sem=more_sems.at[0],
            recv_sem=more_sems.at[1],
            device_id={"clique": 0},
            device_id_type=MESH,
        )
        copy.start()
        copy_slots(old_slots, slots)
        copy.wait_send()

    @pl.when(me == 0)
    def _():
        for k in range(4):
            slots[0, k] = outgoing[k]
        pltpu.make_async_remote_copy(
            src_ref=incoming.at[pl.ds(1, PIECES - 1)],
            dst_ref=incoming.at[pl.ds(1, PIECES - 1)],
            send_sem=more_sems.at[0],
            recv_sem=more_sems.at[1],
            device_id={"clique": 1},
            device_id_type=MESH,
        ).wait_recv()

        def body(piece, carry):
            for k in range(4):
                slots[piece, k] = incoming[piece, k]
            return carry

        lax.fori_loop(1, PIECES, body, 0)


def send_received(me, outgoing, received, incoming, sems):
    send_pieces(me, outgoing, incoming, sems)
    incoming[me] = outgoing[me]
    all_but_one(me, outgoing, incoming, sems).wait()

    def body(piece, carry):
        received[piece] = incoming[piece]
        return carry

    lax.fori_loop(0, PIECES, body, 0)


def root_spread_kernel(info, margins, received, arrived, outgoing, incoming, sems, more_sems):
    me = lax.axis_index("clique")
    enter(me)

    @pl.when(me == 0)
    def _():
        def body(other, carry):
            pltpu.make_async_remote_copy(
                src_ref=margins.at[other],
                dst_ref=arrived,
                send_sem=sems.at[0],
                recv_sem=sems.at[1],
                device_id={"clique": other},
                device_id_type=MESH,
            ).start()
            return carry

        lax.fori_loop(1, PIECES, body, 0)
        for k in range(4):
            arrived[k] = margins[0, k]

    @pl.when(me != 0)
    def _():
        pltpu.make_async_remote_copy(
            src_ref=arrived,
            dst_ref=arrived,
            send_sem=sems.at[0],
            recv_sem=sems.at[1],
            device_id={"clique": 0},
            device_id_type=MESH,
        ).wait_recv()

    for c in range(PIECES):
        outgoing[c] = arrived[info[SOURCE + c] % 4]
    send_received(me, outgoing, received, incoming, more_sems)

    @pl.when(me == 0)
    def _():
        pltpu.make_async_remote_copy(
            src_ref=margins.at[pl.ds(1, PIECES - 1)],
            dst_ref=margins.at[pl.ds(1, PIECES - 1)],
            send_sem=sems.at[0],
            recv_sem=sems.at[1],
            device_id={"clique": 1},
            device_id_type=MESH,
        ).wait_send()


def spread_kernel(info, margins, received, arrived, outgoing, incoming, sems, more_sems):
    me = lax.axis_index("clique")
    enter(me)
    send_pieces(me, margins, arrived, sems)
    arrived[me] = margins[me]
    all_but_one(me, margins, arrived, sems).wait_recv()
    for c in range(PIECES):
        outgoing[c] = arrived[info[SOURCE + c] // 4, info[SOURCE + c] % 4]
    send_received(me, outgoing, received, incoming, more_sems)
    all_but_one(me, margins, arrived, sems).wait_send()


MESSAGE = jax.ShapeDtypeStruct((PIECES, 8, 128), F32)
SLOTS = jax.ShapeDtypeStruct((PIECES, 4, 8, 128), F32)
TABLE = jax.ShapeDtypeStruct((1024, 1024), F32)
ANY_SPEC = pl.BlockSpec(memory_space=pl.ANY)
S_SPEC = pl.BlockSpec(memory_space=SMEM)
V_SPEC = pl.BlockSpec(memory_space=VMEM)
HELD_MESSAGE = VMEM((PIECES, 8, 128), F32)
HELD_SUMS = VMEM((PIECES + 1, 8, 128), F32)
HELD_SLOTS = VMEM((PIECES, 4, 8, 128), F32)
HELD_PIECE = VMEM((4, 8, 128), F32)
HELD_TABLE = VMEM((1024, 1024), F32)
WORK = [VMEM((1024, 128), F32), VMEM((1024, 128), F32), VMEM((8, 32, 128), F32)]
PAIR_SEMS = pltpu.SemaphoreType.DMA((2,))


def call(kernel, name, ins, outs, out_specs, scratch, collective=None, limit=20):
    more = {} if collective is None else dict(collective_id=collective, has_side_effects=True)
    return pl.pallas_call(
        kernel,
        name=name,
        in_specs=ins,
        out_shape=outs,
        out_specs=out_specs,
        scratch_shapes=scratch,
        compiler_params=pltpu.CompilerParams(vmem_limit_bytes=limit * 2**20, **more),
    )


def per_device(potentials, parent, child_drop, parent_drop):
    table = potentials.reshape(1024, 1024)
    trees = jnp.concatenate([child_drop, parent_drop, parent])
    message, info = call(
        first_kernel,
        "first",
        [ANY_SPEC] * 2,
        (MESSAGE, jax.ShapeDtypeStruct((INFO,), jnp.int32)),
        (V_SPEC, S_SPEC),
        [HELD_TABLE, SMEM((9, 32), jnp.int32)]
        + WORK
        + [pltpu.SemaphoreType.DMA((CHUNKS,)), pltpu.SemaphoreType.DMA],
        limit=53,
    )(trees, table)
    slots = call(
        sums_kernel,
        "sums",
        [S_SPEC, V_SPEC],
        SLOTS,
        V_SPEC,
        [HELD_MESSAGE, HELD_SUMS, HELD_SLOTS, HELD_SLOTS, PAIR_SEMS, PAIR_SEMS],
        collective=0,
    )(info, message)
    message = call(
        up_kernel, "up", [S_SPEC] + [V_SPEC] * 2, MESSAGE, V_SPEC, [HELD_TABLE] + WORK
    )(info, table, slots)
    slots = call(
        root_sums_kernel,
        "root_sums",
        [S_SPEC] + [V_SPEC] * 2,
        SLOTS,
        V_SPEC,
        [HELD_MESSAGE, HELD_SUMS, HELD_PIECE, HELD_SLOTS, PAIR_SEMS, PAIR_SEMS],
        collective=1,
    )(info, message, slots)
    axes = ("clique", "subtree")
    sent, table = call(
        chain_first_kernel, "chain_1", [S_SPEC] + [V_SPEC] * 2, (MESSAGE, TABLE), (V_SPEC, V_SPEC), WORK
    )(info, table, slots)
    first = lax.ppermute(sent, axes, ((3, 2), (0, 1)))
    sent = call(
        functools.partial(chain_kernel, 2),
        "chain_2",
        [S_SPEC] + [V_SPEC] * 2,
        MESSAGE,
        V_SPEC,
        [HELD_TABLE] + WORK,
    )(info, table, first)
    second = lax.ppermute(sent, axes, ((2, 1), (1, 2)))
    sent, table = call(
        functools.partial(chain_kernel, 3),
        "chain_3",
        [S_SPEC] + [V_SPEC] * 2,
        (MESSAGE, TABLE),
        (V_SPEC, V_SPEC),
        WORK,
    )(info, table, second)
    third = lax.ppermute(sent, axes, ((1, 0), (2, 3)))
    margins, table = call(
        root_margins_kernel,
        "root_margins",
        [S_SPEC] + [V_SPEC] * 3,
        (SLOTS, TABLE),
        (V_SPEC, V_SPEC),
        [HELD_MESSAGE] + WORK,
    )(info, table, first, third)
    received = call(
        root_spread_kernel,
        "root_spread",
        [S_SPEC, V_SPEC],
        MESSAGE,
        V_SPEC,
        [HELD_PIECE, HELD_MESSAGE, HELD_MESSAGE, PAIR_SEMS, PAIR_SEMS],
        collective=2,
    )(info, margins)
    margins = call(
        child_margins_kernel,
        "child_margins",
        [S_SPEC] + [V_SPEC] * 3,
        SLOTS,
        V_SPEC,
        [HELD_TABLE, HELD_MESSAGE] + WORK,
    )(info, table, received, message)
    received = call(
        spread_kernel,
        "spread",
        [S_SPEC, V_SPEC],
        MESSAGE,
        V_SPEC,
        [HELD_SLOTS, HELD_MESSAGE, HELD_MESSAGE, PAIR_SEMS, PAIR_SEMS],
        collective=3,
    )(info, margins)
    out = call(
        final_kernel,
        "final",
        [S_SPEC] + [V_SPEC] * 3,
        TABLE,
        ANY_SPEC,
        [HELD_TABLE, HELD_MESSAGE, pltpu.SemaphoreType.DMA((4,))],
    )(info, table, received, message)
    return out.reshape(1, 1, 1024, 1024)


def solution(mesh):
    specs = (P("subtree", "clique", None, None), P("subtree", None), P(), P())
    return jax.shard_map(
        per_device,
        mesh=mesh,
        in_specs=specs,
        out_specs=P("subtree", "clique", None, None),
        check_vma=False,
    )
```

```python
import functools

import jax
import jax.numpy as jnp
from jax import lax
from jax.experimental import pallas as pl
from jax.experimental.pallas import tpu as pltpu
from jax.sharding import PartitionSpec as P

PIECES = 32
CHUNKS = 8
MESH = pl.DeviceIdType.MESH
F32 = jnp.float32
VMEM = pltpu.VMEM
SMEM = pltpu.SMEM


def lanes():
    return lax.broadcasted_iota(jnp.int32, (8, 128), 1)


def rows():
    return lax.broadcasted_iota(jnp.int32, (8, 128), 0)


def take(vec, index):
    return jnp.take_along_axis(vec, index, axis=1, mode="promise_in_bounds")


def tree(parts, op):
    parts = list(parts)
    while len(parts) > 1:
        parts = [op(*parts[n : n + 2]) if n + 1 < len(parts) else parts[n] for n in range(0, len(parts), 2)]
    return parts[0]


def tile(table, a0, i, t):
    return table[pl.ds(pl.multiple_of(a0 * 32 + 8 * i, 8), 8), 128 * t : 128 * (t + 1)]


def prepare_place(hot):
    row = lax.broadcasted_iota(jnp.int32, (256, 1024), 0)
    column = lax.broadcasted_iota(jnp.int32, (256, 1024), 1)
    level = jnp.where(row < 128, column // 32, column % 32)
    hot[...] = jnp.where((level == row % 32) & (row % 128 < 96), 1.0, 0.0).astype(jnp.bfloat16)


def three_parts(vec):
    high = vec.astype(jnp.bfloat16).astype(F32)
    rest = vec - high
    middle = rest.astype(jnp.bfloat16).astype(F32)
    group = lanes() // 32
    return jnp.where(group == 0, high, jnp.where(group == 1, middle, jnp.where(group == 2, rest - middle, 0.0)))


def place(source, target, terms, tools, after=None):
    left, hot = tools
    lane, row = lanes(), rows()
    spread = (row % 4) * 32 + lane % 32
    by_matrix = [k for k in (3, 2) if k in terms] if 3 in terms else []
    depth = 128 * len(by_matrix)

    def body(part, carry):
        def levels(k, s, i):
            read = terms[k][1]
            return take(jnp.where(row < 4, read(part * 8 + 2 * i, s), read(part * 8 + 2 * i + 1, s)), spread)

        if by_matrix:
            for s in range(8):
                for half in range(2):
                    both = [
                        jnp.concatenate([three_parts(levels(k, s, i)) for k in by_matrix], axis=1)
                        for i in (2 * half, 2 * half + 1)
                    ]
                    at = 32 * s + 16 * half
                    left[at : at + 16, :depth] = jnp.concatenate(both, axis=0).astype(jnp.bfloat16)
        for n in range(4):
            if by_matrix:
                back = jnp.dot(
                    left[:, :depth], hot[:depth, 256 * n : 256 * (n + 1)], preferred_element_type=F32
                )
            for s in range(8):
                a0 = part * 8 + s
                third = [levels(2, s, i) for i in range(4)] if 2 in terms and not by_matrix else None
                for t in (2 * n, 2 * n + 1):
                    second = terms[1][1](part * 8 + t, s) if 1 in terms else None
                    for i in range(4):
                        adds = []
                        if 0 in terms:
                            adds.append(terms[0][0](i * 8 + t))
                        if 1 in terms:
                            adds.append(jnp.broadcast_to(second, (8, 128)))
                        if third is not None:
                            adds.append(third[i])
                        if by_matrix:
                            at, column = 32 * s + 8 * i, 128 * (t - 2 * n)
                            adds.append(back[at : at + 8, column : column + 128])
                        where = pl.ds(pl.multiple_of(a0 * 32 + 8 * i, 8), 8)
                        value = tile(source, a0, i, t) + functools.reduce(jnp.add, adds)
                        target[where, 128 * t : 128 * (t + 1)] = value
        if after is not None:
            after(part)
        return carry

    lax.fori_loop(0, 4, body, 0)


def place_slots(source, target, slots, tools, after=None):
    def readers(k):
        return lambda piece: slots[piece, k], lambda piece, s: slots[piece, k, pl.ds(s, 1), :]

    prepare_place(tools[1])
    place(source, target, {k: readers(k) for k in range(4)}, tools, after)


def place_message(source, target, message, axis, tools, after=None):
    for k in range(4):

        @pl.when(axis == k)
        def _(k=k):
            readers = (lambda piece: message[piece], lambda piece, s: message[piece, pl.ds(s, 1), :])
            if k == 3:
                prepare_place(tools[1])
            place(source, target, {k: readers}, tools, after)


def pick(parts):
    group = lanes() // 32
    return jnp.where(
        group == 0, parts[0], jnp.where(group == 1, parts[1], jnp.where(group == 2, parts[2], parts[3]))
    )


def margin_0(table, put, work):
    def body(i, carry):
        for t in range(8):
            parts = [tile(table, a0, i, t) for a0 in range(32)]
            top = tree(parts, jnp.maximum)
            total = tree([jnp.exp(part - top) for part in parts], jnp.add)
            put(i * 8 + t, 1, None, top + jnp.log(total))
        return carry

    lax.fori_loop(0, 4, body, 0)


def over_rows(vec, op):
    for shift in (4, 2, 1):
        vec = op(vec, pltpu.roll(vec, shift, 0))
    return vec


def margin_1(table, put, work):
    def body(a0, carry):
        for t in range(8):
            parts = [tile(table, a0, i, t) for i in range(4)]
            top = over_rows(tree(parts, jnp.maximum), jnp.maximum)
            total = over_rows(tree([jnp.exp(part - top) for part in parts], jnp.add), jnp.add)
            put((a0 // 8) * 8 + t, 1, a0 % 8, (top + jnp.log(total))[0:1])
        return carry

    lax.fori_loop(0, 32, body, 0)


def margin_2(table, put, work):
    totals, tops = work[0], work[1]

    def largest(a0, carry):
        for i in range(4):
            at = pl.ds(pl.multiple_of((a0 * 4 + i) * 8, 8), 8)
            totals[at, :] = tree([tile(table, a0, i, t) for t in range(8)], jnp.maximum)
        return carry

    lax.fori_loop(0, 32, largest, 0, unroll=4)

    def groups(n, carry):
        ats = [pl.ds(pl.multiple_of((n * 32 + m) * 8, 8), 8) for m in range(32)]
        parts = [totals[at, :] for at in ats]
        for shift in (64, 32):
            moved = [pltpu.roll(part, shift, 1) for part in parts]
            parts = [jnp.maximum(part, other) for part, other in zip(parts, moved)]
        for at, part in zip(ats, parts):
            tops[at, :] = part
        return carry

    lax.fori_loop(0, 4, groups, 0)

    def sums(a0, carry):
        for i in range(4):
            at = pl.ds(pl.multiple_of((a0 * 4 + i) * 8, 8), 8)
            top = tops[at, :]
            totals[at, :] = tree([jnp.exp(tile(table, a0, i, t) - top) for t in range(8)], jnp.add)
        return carry

    lax.fori_loop(0, 32, sums, 0, unroll=2)

    def pack(part, carry):
        packed = []
        for s in range(8):
            start = (part * 8 + s) * 32
            total = [totals[pl.ds(start + q, 8, stride=4), :] for q in range(4)]
            top = pick([tops[pl.ds(start + q, 8, stride=4), :] for q in range(4)])
            turned = [pick([total[(g + r) % 4] for g in range(4)]) for r in range(4)]
            packed.append((top, [turned[0]] + [pltpu.roll(turned[r], 32 * r, 1) for r in range(1, 4)]))
        for s, (top, turned) in enumerate(packed):
            put(part * 8, 8, s, top + jnp.log((turned[0] + turned[1]) + (turned[2] + turned[3])))
        return carry

    lax.fori_loop(0, 4, pack, 0)


def margin_3(table, put, work):
    flat, across = work[0], work[2]

    def body(block, carry):
        for t in range(8):
            turned = table[pl.ds(pl.multiple_of(block * 128, 128), 128), 128 * t : 128 * (t + 1)].T
            for g in range(4):
                parts = [turned[32 * g + 8 * m : 32 * g + 8 * (m + 1)] for m in range(4)]
                top = over_rows(tree(parts, jnp.maximum), jnp.maximum)
                total = over_rows(tree([jnp.exp(part - top) for part in parts], jnp.add), jnp.add)
                across[block, 4 * t + g : 4 * t + g + 1, :] = (top + jnp.log(total))[0:1]
        return carry

    lax.fori_loop(0, 8, body, 0, unroll=2)
    for block in range(8):
        part = across[block]
        flat[128 * block : 128 * (block + 1), :] = jnp.concatenate([part] * 4, axis=0).T
    for a0 in range(32):
        put((a0 // 8) * 8, 8, a0 % 8, pick([flat[pl.ds(a0 * 32 + q, 8, stride=4), :] for q in range(4)]))


MARGINS = (margin_0, margin_1, margin_2, margin_3)


def message_put(message):
    def put(piece, count, row, value):
        if row is None:
            message[piece] = value
        elif count == 1:
            message[piece, pl.ds(row, 1), :] = value
        else:
            message[pl.ds(piece, count), row, :] = value

    return put


def slot_put(slots, k):
    def put(piece, count, row, value):
        if row is None:
            slots[piece, k] = value
        elif count == 1:
            slots[piece, k, pl.ds(row, 1), :] = value
        else:
            slots[pl.ds(piece, count), k, row, :] = value

    return put


def chosen_margin(table, axis, message, work):
    for k in range(4):

        @pl.when(axis == k)
        def _(k=k):
            MARGINS[k](table, message_put(message), work)


def copy_slots(source, target):
    def body(piece, carry):
        for k in range(4):
            target[piece, k] = source[piece, k]
        return carry

    lax.fori_loop(0, PIECES, body, 0)


PREVIOUS, LAST, SOURCE, OWN_DROP, CHAIN_AXIS, CHAIN_SLOT, INFO = 0, 32, 160, 192, 192, 196, 256


def first_kernel(trees_in, potentials, message, info, table, trees, *rest):
    work, load_sems, sems = rest[:5], rest[5], rest[6]
    me, s = lax.axis_index("clique"), lax.axis_index("subtree")
    size = 1024 // CHUNKS
    loads = [
        pltpu.make_async_copy(
            potentials.at[pl.ds(size * n, size)], table.at[pl.ds(size * n, size)], load_sems.at[n]
        )
        for n in range(CHUNKS)
    ]
    small = pltpu.make_async_copy(trees_in, trees, sems)
    small.start()
    for copy in loads:
        copy.start()
    for n in range(128):
        info[LAST + n] = PIECES
    small.wait()
    info[PREVIOUS] = PIECES
    info[SOURCE] = trees[4 + s, 0]

    def link(c, carry):
        target = trees[8, c] * 4 + trees[4 + s, c]
        info[SOURCE + c] = target
        info[PREVIOUS + c] = info[LAST + target]
        info[LAST + target] = c
        return carry

    lax.fori_loop(1, PIECES, link, 0)
    own = trees[s, me]
    info[OWN_DROP] = own
    to_next = trees[4 + jnp.minimum(s + 1, 3), 0]
    to_previous = trees[s, 0]
    for step, sender, receiver in ((1, 0, 2), (2, 1, 1), (3, 2, 0)):
        info[CHAIN_AXIS + step] = jnp.where(s == sender, to_next, to_previous)
        info[CHAIN_SLOT + step] = jnp.where(s == receiver, to_next, to_previous)
    for copy in loads:
        copy.wait()
    chosen_margin(table, own, message, work)


def up_kernel(info, table, slots, message, placed, *work):
    place_slots(table, placed, slots, work[3:])
    chosen_margin(placed, info[OWN_DROP], message, work)


def chain_first_kernel(info, table, slots, message, placed, *work):
    place_slots(table, placed, slots, work[3:])
    chosen_margin(placed, info[CHAIN_AXIS + 1], message, work)


def chain_kernel(step, info, table, arrived, message, placed, *work):
    place_message(table, placed, arrived, info[CHAIN_SLOT + step - 1], work[3:])
    chosen_margin(placed, info[CHAIN_AXIS + step], message, work)


def last_root_slot(info):
    s = lax.axis_index("subtree")
    inner = (s == 1) | (s == 2)
    return inner, jnp.where(inner, info[CHAIN_SLOT + 1], info[CHAIN_SLOT + 3])


def final_kernel(info, table, first, third, received, message, out, belief, held, left, hot, sems):
    below = lax.axis_index("clique") != 0
    inner, slot = last_root_slot(info)
    top = jnp.max(tree([received[piece] for piece in range(PIECES)], jnp.maximum))
    total = tree([jnp.exp(received[piece] - top) for piece in range(PIECES)], jnp.add)
    log_total = top + jnp.log(jnp.broadcast_to(jnp.sum(total), (8, 128)))
    for piece in range(PIECES):
        at_root = jnp.where(inner, first[piece], third[piece])
        held[piece] = jnp.where(below, received[piece] - message[piece], at_root) - log_total

    def out_copy(part):
        at = pl.ds(pl.multiple_of(part * 256, 256), 256)
        return pltpu.make_async_copy(belief.at[at], out.at[at], sems.at[part])

    axis = jnp.where(below, info[OWN_DROP], slot)
    place_message(table, belief, held, axis, (left, hot), after=lambda part: out_copy(part).start())
    for part in range(4):
        out_copy(part).wait()


def announce(me):
    barrier = pltpu.get_barrier_semaphore()

    def body(d, carry):
        pl.semaphore_signal(barrier, inc=1, device_id={"clique": (me + d) % PIECES}, device_id_type=MESH)
        return carry

    lax.fori_loop(1, PIECES, body, 0)


def await_others():
    pl.semaphore_wait(pltpu.get_barrier_semaphore(), PIECES - 1)


def enter(me):
    announce(me)
    await_others()


def send_pieces(me, source, target, sems):
    def body(d, carry):
        other = (me + d) % PIECES
        pltpu.make_async_remote_copy(
            src_ref=source.at[other],
            dst_ref=target.at[me],
            send_sem=sems.at[0],
            recv_sem=sems.at[1],
            device_id={"clique": other},
            device_id_type=MESH,
        ).start()
        return carry

    lax.fori_loop(1, PIECES, body, 0)


def all_but_one(me, source, target, sems):
    return pltpu.make_async_remote_copy(
        src_ref=source.at[pl.ds(0, PIECES - 1)],
        dst_ref=target.at[pl.ds(0, PIECES - 1)],
        send_sem=sems.at[0],
        recv_sem=sems.at[1],
        device_id={"clique": (me + 1) % PIECES},
        device_id_type=MESH,
    )


def gather_up(me, info, message, arrived, sums, sems):
    enter(me)
    send_pieces(me, message, arrived, sems)
    arrived[me] = message[me]
    all_but_one(me, message, arrived, sems).wait_recv()
    sums[PIECES] = jnp.zeros((8, 128), F32)
    for c in range(1, PIECES):
        sums[c] = arrived[c] + sums[info[PREVIOUS + c]]
    all_but_one(me, message, arrived, sems).wait_send()


def sums_kernel(info, message, slots, arrived, sums, outgoing, incoming, sems, more_sems):
    me = lax.axis_index("clique")
    gather_up(me, info, message, arrived, sums, sems)

    def body(p, carry):
        for k in range(4):
            outgoing[p, k] = sums[info[LAST + p * 4 + k]]
        return carry

    lax.fori_loop(0, PIECES, body, 0)
    send_pieces(me, outgoing, incoming, more_sems)
    incoming[me] = outgoing[me]
    all_but_one(me, outgoing, incoming, more_sems).wait()
    copy_slots(incoming, slots)


def root_sums_kernel(info, message, old_slots, slots, arrived, sums, outgoing, incoming, sems, more_sems):
    me = lax.axis_index("clique")
    gather_up(me, info, message, arrived, sums, sems)
    for k in range(4):
        outgoing[k] = sums[info[LAST + k]]

    @pl.when(me != 0)
    def _():
        copy = pltpu.make_async_remote_copy(
            src_ref=outgoing,
            dst_ref=incoming.at[me],
            send_sem=more_sems.at[0],
            recv_sem=more_sems.at[1],
            device_id={"clique": 0},
            device_id_type=MESH,
        )
        copy.start()
        copy_slots(old_slots, slots)
        copy.wait_send()

    @pl.when(me == 0)
    def _():
        for k in range(4):
            slots[0, k] = outgoing[k]
        pltpu.make_async_remote_copy(
            src_ref=incoming.at[pl.ds(1, PIECES - 1)],
            dst_ref=incoming.at[pl.ds(1, PIECES - 1)],
            send_sem=more_sems.at[0],
            recv_sem=more_sems.at[1],
            device_id={"clique": 1},
            device_id_type=MESH,
        ).wait_recv()

        def body(piece, carry):
            for k in range(4):
                slots[piece, k] = incoming[piece, k]
            return carry

        lax.fori_loop(1, PIECES, body, 0)


def send_slot(me, k, source, target, sems):
    def body(d, carry):
        other = (me + d) % PIECES
        pltpu.make_async_remote_copy(
            src_ref=source.at[other, k],
            dst_ref=target.at[me, k],
            send_sem=sems.at[0],
            recv_sem=sems.at[1],
            device_id={"clique": other},
            device_id_type=MESH,
        ).start()
        return carry

    lax.fori_loop(1, PIECES, body, 0)


def part_of(me, count, source, target, sems):
    return pltpu.make_async_remote_copy(
        src_ref=source.at[pl.ds(0, count)],
        dst_ref=target.at[pl.ds(0, count)],
        send_sem=sems.at[0],
        recv_sem=sems.at[1],
        device_id={"clique": (me + 1) % PIECES},
        device_id_type=MESH,
    )


def down_kernel(info, table, first, third, message, received, *scratch):
    belief, margins, held, arrived, out_1, in_1, out_2, in_2 = scratch[:8]
    work, sems = scratch[8:13], scratch[13:]
    me = lax.axis_index("clique")
    announce(me)

    def send_margins(pair):
        for k in (2, 1, 3, 0):
            MARGINS[k](belief, slot_put(margins, k), work)
            send_slot(me, k, margins, arrived, pair)
        for k in range(4):
            arrived[me, k] = margins[me, k]

    @pl.when(me == 0)
    def _():
        inner, slot = last_root_slot(info)

        def body(piece, carry):
            value = jnp.where(inner, first[piece], third[piece])
            for k in range(4):
                held[piece, k] = jnp.where(slot == k, value, 0.0)
            return carry

        lax.fori_loop(0, PIECES, body, 0)
        place_slots(table, belief, held, work[3:])

    await_others()

    @pl.when(me == 0)
    def _():
        send_margins(sems[0])

    @pl.when(me != 0)
    def _():
        part_of(me, 1, margins, arrived, sems[0]).wait_recv()

    for c in range(PIECES):
        out_1[c] = arrived[0, info[SOURCE + c] % 4]
    send_pieces(me, out_1, in_1, sems[1])
    in_1[me] = out_1[me]
    all_but_one(me, out_1, in_1, sems[1]).wait()

    @pl.when(me != 0)
    def _():
        drop = info[OWN_DROP]

        def body(piece, carry):
            value = in_1[piece] - message[piece]
            for k in range(4):
                held[piece, k] = jnp.where(drop == k, value, 0.0)
            return carry

        lax.fori_loop(0, PIECES, body, 0)
        place_slots(table, belief, held, work[3:])
        send_margins(sems[2])
        part_of(me, PIECES - 2, margins, arrived, sems[2]).wait_recv()

    @pl.when(me == 0)
    def _():
        part_of(me, PIECES - 1, margins, arrived, sems[2]).wait_recv()

    for c in range(PIECES):
        out_2[c] = arrived[info[SOURCE + c] // 4, info[SOURCE + c] % 4]
    send_pieces(me, out_2, in_2, sems[3])
    in_2[me] = out_2[me]
    all_but_one(me, out_2, in_2, sems[3]).wait()

    def body(piece, carry):
        received[piece] = in_2[piece]
        return carry

    lax.fori_loop(0, PIECES, body, 0)

    @pl.when(me == 0)
    def _():
        part_of(me, PIECES - 1, margins, arrived, sems[0]).wait_send()

    @pl.when(me != 0)
    def _():
        part_of(me, PIECES - 1, margins, arrived, sems[2]).wait_send()


MESSAGE = jax.ShapeDtypeStruct((PIECES, 8, 128), F32)
SLOTS = jax.ShapeDtypeStruct((PIECES, 4, 8, 128), F32)
TABLE = jax.ShapeDtypeStruct((1024, 1024), F32)
ANY_SPEC = pl.BlockSpec(memory_space=pl.ANY)
S_SPEC = pl.BlockSpec(memory_space=SMEM)
V_SPEC = pl.BlockSpec(memory_space=VMEM)
HELD_MESSAGE = VMEM((PIECES, 8, 128), F32)
HELD_SUMS = VMEM((PIECES + 1, 8, 128), F32)
HELD_SLOTS = VMEM((PIECES, 4, 8, 128), F32)
HELD_PIECE = VMEM((4, 8, 128), F32)
HELD_TABLE = VMEM((1024, 1024), F32)
PLACE_TOOLS = [VMEM((256, 256), jnp.bfloat16), VMEM((256, 1024), jnp.bfloat16)]
WORK = [VMEM((1024, 128), F32), VMEM((1024, 128), F32), VMEM((8, 32, 128), F32)] + PLACE_TOOLS
PAIR_SEMS = pltpu.SemaphoreType.DMA((2,))


def call(kernel, name, ins, outs, out_specs, scratch, collective=None, limit=20):
    more = {} if collective is None else dict(collective_id=collective, has_side_effects=True)
    return pl.pallas_call(
        kernel,
        name=name,
        in_specs=ins,
        out_shape=outs,
        out_specs=out_specs,
        scratch_shapes=scratch,
        compiler_params=pltpu.CompilerParams(vmem_limit_bytes=limit * 2**20, **more),
    )


def per_device(potentials, parent, child_drop, parent_drop):
    table = potentials.reshape(1024, 1024)
    trees = jnp.concatenate([child_drop, parent_drop, parent])
    message, info = call(
        first_kernel,
        "first",
        [ANY_SPEC] * 2,
        (MESSAGE, jax.ShapeDtypeStruct((INFO,), jnp.int32)),
        (V_SPEC, S_SPEC),
        [HELD_TABLE, SMEM((9, 32), jnp.int32)]
        + WORK
        + [pltpu.SemaphoreType.DMA((CHUNKS,)), pltpu.SemaphoreType.DMA],
        limit=53,
    )(trees, table)
    slots = call(
        sums_kernel,
        "sums",
        [S_SPEC, V_SPEC],
        SLOTS,
        V_SPEC,
        [HELD_MESSAGE, HELD_SUMS, HELD_SLOTS, HELD_SLOTS, PAIR_SEMS, PAIR_SEMS],
        collective=0,
    )(info, message)
    message = call(
        up_kernel, "up", [S_SPEC] + [V_SPEC] * 2, MESSAGE, V_SPEC, [HELD_TABLE] + WORK
    )(info, table, slots)
    slots = call(
        root_sums_kernel,
        "root_sums",
        [S_SPEC] + [V_SPEC] * 2,
        SLOTS,
        V_SPEC,
        [HELD_MESSAGE, HELD_SUMS, HELD_PIECE, HELD_SLOTS, PAIR_SEMS, PAIR_SEMS],
        collective=1,
    )(info, message, slots)
    axes = ("clique", "subtree")
    sent, table = call(
        chain_first_kernel, "chain_1", [S_SPEC] + [V_SPEC] * 2, (MESSAGE, TABLE), (V_SPEC, V_SPEC), WORK
    )(info, table, slots)
    first = lax.ppermute(sent, axes, ((3, 2), (0, 1)))
    sent = call(
        functools.partial(chain_kernel, 2),
        "chain_2",
        [S_SPEC] + [V_SPEC] * 2,
        MESSAGE,
        V_SPEC,
        [HELD_TABLE] + WORK,
    )(info, table, first)
    second = lax.ppermute(sent, axes, ((2, 1), (1, 2)))
    sent, table = call(
        functools.partial(chain_kernel, 3),
        "chain_3",
        [S_SPEC] + [V_SPEC] * 2,
        (MESSAGE, TABLE),
        (V_SPEC, V_SPEC),
        WORK,
    )(info, table, second)
    third = lax.ppermute(sent, axes, ((1, 0), (2, 3)))
    received = call(
        down_kernel,
        "down",
        [S_SPEC] + [V_SPEC] * 4,
        MESSAGE,
        V_SPEC,
        [HELD_TABLE] + [HELD_SLOTS] * 3 + [HELD_MESSAGE] * 4 + WORK + [PAIR_SEMS] * 4,
        collective=2,
    )(info, table, first, third, message)
    out = call(
        final_kernel,
        "final",
        [S_SPEC] + [V_SPEC] * 5,
        TABLE,
        ANY_SPEC,
        [HELD_TABLE, HELD_MESSAGE] + PLACE_TOOLS + [pltpu.SemaphoreType.DMA((4,))],
    )(info, table, first, third, received, message)
    return out.reshape(1, 1, 1024, 1024)


def solution(mesh):
    specs = (P("subtree", "clique", None, None), P("subtree", None), P(), P())
    return jax.shard_map(
        per_device,
        mesh=mesh,
        in_specs=specs,
        out_specs=P("subtree", "clique", None, None),
        check_vma=False,
    )
```

```python
import functools

import jax
import jax.numpy as jnp
from jax import lax
from jax.experimental import pallas as pl
from jax.experimental.pallas import tpu as pltpu
from jax.sharding import PartitionSpec as P

PIECES = 32
CHUNKS = 8
MESH = pl.DeviceIdType.MESH
F32 = jnp.float32
VMEM = pltpu.VMEM
SMEM = pltpu.SMEM


def lanes():
    return lax.broadcasted_iota(jnp.int32, (8, 128), 1)


def rows():
    return lax.broadcasted_iota(jnp.int32, (8, 128), 0)


def take(vec, index):
    return jnp.take_along_axis(vec, index, axis=1, mode="promise_in_bounds")


def tree(parts, op):
    parts = list(parts)
    while len(parts) > 1:
        parts = [op(*parts[n : n + 2]) if n + 1 < len(parts) else parts[n] for n in range(0, len(parts), 2)]
    return parts[0]


def tile(table, a0, i, t):
    return table[pl.ds(pl.multiple_of(a0 * 32 + 8 * i, 8), 8), 128 * t : 128 * (t + 1)]


def prepare_place(hot):
    row = lax.broadcasted_iota(jnp.int32, (256, 1024), 0)
    column = lax.broadcasted_iota(jnp.int32, (256, 1024), 1)
    level = jnp.where(row < 128, column // 32, column % 32)
    hot[...] = jnp.where((level == row % 32) & (row % 128 < 96), 1.0, 0.0).astype(jnp.bfloat16)


def three_parts(vec):
    high = vec.astype(jnp.bfloat16).astype(F32)
    rest = vec - high
    middle = rest.astype(jnp.bfloat16).astype(F32)
    group = lanes() // 32
    return jnp.where(group == 0, high, jnp.where(group == 1, middle, jnp.where(group == 2, rest - middle, 0.0)))


def place(source, target, terms, tools, after=None):
    left, hot = tools
    lane, row = lanes(), rows()
    spread = (row % 4) * 32 + lane % 32
    by_matrix = [k for k in (3, 2) if k in terms] if 3 in terms else []
    depth = 128 * len(by_matrix)

    def body(part, carry):
        def levels(k, s, i):
            read = terms[k][1]
            return take(jnp.where(row < 4, read(part * 8 + 2 * i, s), read(part * 8 + 2 * i + 1, s)), spread)

        if by_matrix:
            for s in range(8):
                for half in range(2):
                    both = [
                        jnp.concatenate([three_parts(levels(k, s, i)) for k in by_matrix], axis=1)
                        for i in (2 * half, 2 * half + 1)
                    ]
                    at = 32 * s + 16 * half
                    left[at : at + 16, :depth] = jnp.concatenate(both, axis=0).astype(jnp.bfloat16)
        for n in range(4):
            if by_matrix:
                back = jnp.dot(
                    left[:, :depth], hot[:depth, 256 * n : 256 * (n + 1)], preferred_element_type=F32
                )
            for s in range(8):
                a0 = part * 8 + s
                third = [levels(2, s, i) for i in range(4)] if 2 in terms and not by_matrix else None
                for t in (2 * n, 2 * n + 1):
                    second = terms[1][1](part * 8 + t, s) if 1 in terms else None
                    for i in range(4):
                        adds = []
                        if 0 in terms:
                            adds.append(terms[0][0](i * 8 + t))
                        if 1 in terms:
                            adds.append(jnp.broadcast_to(second, (8, 128)))
                        if third is not None:
                            adds.append(third[i])
                        if by_matrix:
                            at, column = 32 * s + 8 * i, 128 * (t - 2 * n)
                            adds.append(back[at : at + 8, column : column + 128])
                        where = pl.ds(pl.multiple_of(a0 * 32 + 8 * i, 8), 8)
                        value = tile(source, a0, i, t) + functools.reduce(jnp.add, adds)
                        target[where, 128 * t : 128 * (t + 1)] = value
        if after is not None:
            after(part)
        return carry

    lax.fori_loop(0, 4, body, 0)


def place_slots(source, target, slots, tools, after=None, prepared=False):
    def readers(k):
        return lambda piece: slots[piece, k], lambda piece, s: slots[piece, k, pl.ds(s, 1), :]

    if not prepared:
        prepare_place(tools[1])
    place(source, target, {k: readers(k) for k in range(4)}, tools, after)


def place_message(source, target, message, axis, tools, after=None):
    for k in range(4):

        @pl.when(axis == k)
        def _(k=k):
            readers = (lambda piece: message[piece], lambda piece, s: message[piece, pl.ds(s, 1), :])
            if k == 3:
                prepare_place(tools[1])
            place(source, target, {k: readers}, tools, after)


def pick(parts):
    group = lanes() // 32
    return jnp.where(
        group == 0, parts[0], jnp.where(group == 1, parts[1], jnp.where(group == 2, parts[2], parts[3]))
    )


def margin_0(table, put, work):
    def body(i, carry):
        for t in range(8):
            parts = [tile(table, a0, i, t) for a0 in range(32)]
            top = tree(parts, jnp.maximum)
            total = tree([jnp.exp(part - top) for part in parts], jnp.add)
            put(i * 8 + t, 1, None, top + jnp.log(total))
        return carry

    lax.fori_loop(0, 4, body, 0)


def over_rows(vec, op):
    for shift in (4, 2, 1):
        vec = op(vec, pltpu.roll(vec, shift, 0))
    return vec


def margin_1(table, put, work):
    def body(a0, carry):
        for t in range(8):
            parts = [tile(table, a0, i, t) for i in range(4)]
            top = over_rows(tree(parts, jnp.maximum), jnp.maximum)
            total = over_rows(tree([jnp.exp(part - top) for part in parts], jnp.add), jnp.add)
            put((a0 // 8) * 8 + t, 1, a0 % 8, (top + jnp.log(total))[0:1])
        return carry

    lax.fori_loop(0, 32, body, 0)


def margin_2(table, put, work):
    totals, tops = work[0], work[1]

    def largest(a0, carry):
        for i in range(4):
            at = pl.ds(pl.multiple_of((a0 * 4 + i) * 8, 8), 8)
            totals[at, :] = tree([tile(table, a0, i, t) for t in range(8)], jnp.maximum)
        return carry

    lax.fori_loop(0, 32, largest, 0, unroll=4)

    def groups(n, carry):
        ats = [pl.ds(pl.multiple_of((n * 32 + m) * 8, 8), 8) for m in range(32)]
        parts = [totals[at, :] for at in ats]
        for shift in (64, 32):
            moved = [pltpu.roll(part, shift, 1) for part in parts]
            parts = [jnp.maximum(part, other) for part, other in zip(parts, moved)]
        for at, part in zip(ats, parts):
            tops[at, :] = part
        return carry

    lax.fori_loop(0, 4, groups, 0)

    def sums(a0, carry):
        for i in range(4):
            at = pl.ds(pl.multiple_of((a0 * 4 + i) * 8, 8), 8)
            top = tops[at, :]
            totals[at, :] = tree([jnp.exp(tile(table, a0, i, t) - top) for t in range(8)], jnp.add)
        return carry

    lax.fori_loop(0, 32, sums, 0, unroll=2)

    def pack(part, carry):
        packed = []
        for s in range(8):
            start = (part * 8 + s) * 32
            total = [totals[pl.ds(start + q, 8, stride=4), :] for q in range(4)]
            top = pick([tops[pl.ds(start + q, 8, stride=4), :] for q in range(4)])
            turned = [pick([total[(g + r) % 4] for g in range(4)]) for r in range(4)]
            packed.append((top, [turned[0]] + [pltpu.roll(turned[r], 32 * r, 1) for r in range(1, 4)]))
        for s, (top, turned) in enumerate(packed):
            put(part * 8, 8, s, top + jnp.log((turned[0] + turned[1]) + (turned[2] + turned[3])))
        return carry

    lax.fori_loop(0, 4, pack, 0)


def margin_3(table, put, work):
    flat, across = work[0], work[2]

    def body(block, carry):
        for t in range(8):
            turned = table[pl.ds(pl.multiple_of(block * 128, 128), 128), 128 * t : 128 * (t + 1)].T
            for g in range(4):
                parts = [turned[32 * g + 8 * m : 32 * g + 8 * (m + 1)] for m in range(4)]
                top = over_rows(tree(parts, jnp.maximum), jnp.maximum)
                total = over_rows(tree([jnp.exp(part - top) for part in parts], jnp.add), jnp.add)
                across[block, 4 * t + g : 4 * t + g + 1, :] = (top + jnp.log(total))[0:1]
        return carry

    lax.fori_loop(0, 8, body, 0, unroll=2)
    for block in range(8):
        part = across[block]
        flat[128 * block : 128 * (block + 1), :] = jnp.concatenate([part] * 4, axis=0).T
    for a0 in range(32):
        put((a0 // 8) * 8, 8, a0 % 8, pick([flat[pl.ds(a0 * 32 + q, 8, stride=4), :] for q in range(4)]))


MARGINS = (margin_0, margin_1, margin_2, margin_3)


def message_put(message):
    def put(piece, count, row, value):
        if row is None:
            message[piece] = value
        elif count == 1:
            message[piece, pl.ds(row, 1), :] = value
        else:
            message[pl.ds(piece, count), row, :] = value

    return put


def slot_put(slots, k):
    def put(piece, count, row, value):
        if row is None:
            slots[piece, k] = value
        elif count == 1:
            slots[piece, k, pl.ds(row, 1), :] = value
        else:
            slots[pl.ds(piece, count), k, row, :] = value

    return put


def chosen_margin(table, axis, message, work):
    for k in range(4):

        @pl.when(axis == k)
        def _(k=k):
            MARGINS[k](table, message_put(message), work)


def copy_slots(source, target):
    def body(piece, carry):
        for k in range(4):
            target[piece, k] = source[piece, k]
        return carry

    lax.fori_loop(0, PIECES, body, 0)


PREVIOUS, LAST, SOURCE, OWN_DROP, CHAIN_AXIS, CHAIN_SLOT, INFO = 0, 32, 160, 192, 192, 196, 256


def first_kernel(trees_in, potentials, message, info, table, trees, *rest):
    work, load_sems, sems = rest[:5], rest[5], rest[6]
    me, s = lax.axis_index("clique"), lax.axis_index("subtree")
    size = 1024 // CHUNKS
    loads = [
        pltpu.make_async_copy(
            potentials.at[pl.ds(size * n, size)], table.at[pl.ds(size * n, size)], load_sems.at[n]
        )
        for n in range(CHUNKS)
    ]
    small = pltpu.make_async_copy(trees_in, trees, sems)
    small.start()
    for copy in loads:
        copy.start()
    for n in range(128):
        info[LAST + n] = PIECES
    small.wait()
    info[PREVIOUS] = PIECES
    info[SOURCE] = trees[4 + s, 0]

    def link(c, carry):
        target = trees[8, c] * 4 + trees[4 + s, c]
        info[SOURCE + c] = target
        info[PREVIOUS + c] = info[LAST + target]
        info[LAST + target] = c
        return carry

    lax.fori_loop(1, PIECES, link, 0)
    own = trees[s, me]
    info[OWN_DROP] = own
    to_next = trees[4 + jnp.minimum(s + 1, 3), 0]
    to_previous = trees[s, 0]
    for step, sender, receiver in ((1, 0, 2), (2, 1, 1), (3, 2, 0)):
        active = (me == 0) & (((s == 1) | (s == 2)) == (step > 1))
        info[CHAIN_AXIS + step] = jnp.where(active, jnp.where(s == sender, to_next, to_previous), 4)
        info[CHAIN_SLOT + step] = jnp.where(s == receiver, to_next, to_previous)
    for copy in loads:
        copy.wait()
    chosen_margin(table, own, message, work)


def up_kernel(info, table, slots, message, placed, *work):
    place_slots(table, placed, slots, work[3:])
    chosen_margin(placed, info[OWN_DROP], message, work)


def chain_first_kernel(info, table, slots, message, placed, *work):
    place_slots(table, placed, slots, work[3:])
    chosen_margin(placed, info[CHAIN_AXIS + 1], message, work)


def chain_kernel(step, info, table, arrived, message, placed, *work):
    place_message(table, placed, arrived, info[CHAIN_SLOT + step - 1], work[3:])
    chosen_margin(placed, info[CHAIN_AXIS + step], message, work)


def inner_root(s):
    return (s == 1) | (s == 2)


def last_root_slot(info):
    inner = inner_root(lax.axis_index("subtree"))
    return jnp.where(inner, info[CHAIN_SLOT + 1], info[CHAIN_SLOT + 3])


def final_kernel(info, table, last_root, received, message, out, belief, held, left, hot, sems):
    below = lax.axis_index("clique") != 0
    top = jnp.max(tree([received[piece] for piece in range(PIECES)], jnp.maximum))
    total = tree([jnp.exp(received[piece] - top) for piece in range(PIECES)], jnp.add)
    log_total = top + jnp.log(jnp.broadcast_to(jnp.sum(total), (8, 128)))
    for piece in range(PIECES):
        held[piece] = jnp.where(below, received[piece] - message[piece], last_root[piece]) - log_total

    def out_copy(part):
        at = pl.ds(pl.multiple_of(part * 256, 256), 256)
        return pltpu.make_async_copy(belief.at[at], out.at[at], sems.at[part])

    axis = jnp.where(below, info[OWN_DROP], last_root_slot(info))
    place_message(table, belief, held, axis, (left, hot), after=lambda part: out_copy(part).start())
    for part in range(4):
        out_copy(part).wait()


TURNS = sorted(
    (turn for turn in range(1, PIECES)),
    key=lambda turn: -(min(turn // 8, 4 - turn // 8) + min(turn // 2 % 4, 4 - turn // 2 % 4)),
)


def turned(me, turn):
    y, z, core = (me // 8 + turn // 8) % 4, (me // 2 % 4 + turn // 2 % 4) % 4, (me % 2 + turn % 2) % 2
    return y * 8 + z * 2 + core


def announce(me):
    barrier = pltpu.get_barrier_semaphore()
    for turn in TURNS:
        pl.semaphore_signal(barrier, inc=1, device_id={"clique": turned(me, turn)}, device_id_type=MESH)


def await_others():
    pl.semaphore_wait(pltpu.get_barrier_semaphore(), PIECES - 1)


def enter(me):
    announce(me)
    await_others()


def send_pieces(me, source, target, sems, prepare=None):
    for turn in TURNS:
        other = turned(me, turn)
        if prepare is not None:
            prepare(other)
        pltpu.make_async_remote_copy(
            src_ref=source.at[other],
            dst_ref=target.at[me],
            send_sem=sems.at[0],
            recv_sem=sems.at[1],
            device_id={"clique": other},
            device_id_type=MESH,
        ).start()


def part_of(me, count, source, target, sems):
    return pltpu.make_async_remote_copy(
        src_ref=source.at[pl.ds(0, count)],
        dst_ref=target.at[pl.ds(0, count)],
        send_sem=sems.at[0],
        recv_sem=sems.at[1],
        device_id={"clique": (me + 1) % PIECES},
        device_id_type=MESH,
    )


def all_but_one(me, source, target, sems):
    return part_of(me, PIECES - 1, source, target, sems)


def gather_up(me, info, message, arrived, sums, sems):
    enter(me)
    send_pieces(me, message, arrived, sems)
    arrived[me] = message[me]
    sums[PIECES] = jnp.zeros((8, 128), F32)
    all_but_one(me, message, arrived, sems).wait_recv()
    for c in range(1, PIECES):
        sums[c] = arrived[c] + sums[info[PREVIOUS + c]]
    all_but_one(me, message, arrived, sems).wait_send()


def sums_kernel(info, message, slots, arrived, sums, outgoing, sems, more_sems):
    me = lax.axis_index("clique")
    gather_up(me, info, message, arrived, sums, sems)

    def prepare(p):
        for k in range(4):
            outgoing[p, k] = sums[info[LAST + p * 4 + k]]

    send_pieces(me, outgoing, slots, more_sems, prepare)
    for k in range(4):
        slots[me, k] = sums[info[LAST + me * 4 + k]]
    all_but_one(me, outgoing, slots, more_sems).wait()


def root_sums_kernel(info, message, old_slots, slots, arrived, sums, outgoing, sems, more_sems):
    me = lax.axis_index("clique")
    gather_up(me, info, message, arrived, sums, sems)

    @pl.when(me != 0)
    def _():
        for k in range(4):
            outgoing[k] = sums[info[LAST + k]]
        copy = pltpu.make_async_remote_copy(
            src_ref=outgoing,
            dst_ref=slots.at[me],
            send_sem=more_sems.at[0],
            recv_sem=more_sems.at[1],
            device_id={"clique": 0},
            device_id_type=MESH,
        )
        copy.start()
        copy_slots(old_slots, slots)
        copy.wait_send()

    @pl.when(me == 0)
    def _():
        for k in range(4):
            slots[0, k] = sums[info[LAST + k]]
        all_but_one(me, slots, slots, more_sems).wait_recv()


def to_root(s, step, source, target, sems):
    partner = 3 - s if step == 2 else s + 1 - 2 * (s % 2)
    return partner, pltpu.make_async_remote_copy(
        src_ref=source,
        dst_ref=target,
        send_sem=sems.at[0],
        recv_sem=sems.at[1],
        device_id={"subtree": partner},
        device_id_type=MESH,
    )


def hop_kernel(step, sent, arrived, sems):
    me, s = lax.axis_index("clique"), lax.axis_index("subtree")
    partner, copy = to_root(s, step, sent, arrived, sems)
    barrier = pltpu.get_barrier_semaphore()
    receives = (me == 0) & inner_root(s)
    sends = (me == 0) & (inner_root(s) == (step == 2))

    @pl.when(receives)
    def _():
        pl.semaphore_signal(barrier, inc=1, device_id={"subtree": partner}, device_id_type=MESH)

    @pl.when(sends)
    def _():
        pl.semaphore_wait(barrier, 1)
        copy.start()

    @pl.when(jnp.logical_not(receives))
    def _():
        for piece in range(PIECES):
            arrived[piece] = jnp.zeros((8, 128), F32)

    @pl.when(receives)
    def _():
        copy.wait_recv()

    @pl.when(sends)
    def _():
        copy.wait_send()


def send_slot(me, k, source, target, sems):
    for turn in TURNS:
        other = turned(me, turn)
        pltpu.make_async_remote_copy(
            src_ref=source.at[other, k],
            dst_ref=target,
            send_sem=sems.at[0],
            recv_sem=sems.at[1],
            device_id={"clique": other},
            device_id_type=MESH,
        ).start()


def down_kernel(info, table, first, sent, message, received, last_root, *scratch):
    belief, margins, held, arrived, from_root, third, out_1, in_1, out_2 = scratch[:9]
    work, sems = scratch[9:14], scratch[14:]
    me, s = lax.axis_index("clique"), lax.axis_index("subtree")
    inner = inner_root(s)
    sends, receives = (me == 0) & inner, (me == 0) & jnp.logical_not(inner)
    partner, copy = to_root(s, 3, sent, third, sems[4])
    barrier = pltpu.get_barrier_semaphore()

    @pl.when(receives)
    def _():
        pl.semaphore_signal(barrier, inc=1, device_id={"subtree": partner}, device_id_type=MESH)

    announce(me)

    @pl.when(sends)
    def _():
        pl.semaphore_wait(barrier, PIECES)
        copy.start()

    @pl.when(jnp.logical_not(sends))
    def _():
        pl.semaphore_wait(barrier, PIECES - 1)

    def send_margins(pair, target):
        for k in (2, 1, 3, 0):
            MARGINS[k](belief, slot_put(margins, k), work)
            send_slot(me, k, margins, target.at[k], pair)
        for k in range(4):
            target[k] = margins[me, k]

    @pl.when(me == 0)
    def _():
        prepare_place(work[4])

    @pl.when(receives)
    def _():
        copy.wait_recv()

        def body(piece, carry):
            last_root[piece] = third[piece]
            return carry

        lax.fori_loop(0, PIECES, body, 0)

    @pl.when(jnp.logical_not(receives))
    def _():
        def body(piece, carry):
            last_root[piece] = first[piece]
            return carry

        lax.fori_loop(0, PIECES, body, 0)

    @pl.when(me == 0)
    def _():
        slot = last_root_slot(info)

        def body(piece, carry):
            for k in range(4):
                held[piece, k] = jnp.where(slot == k, last_root[piece], 0.0)
            return carry

        lax.fori_loop(0, PIECES, body, 0)
        place_slots(table, belief, held, work[3:], prepared=True)
        send_margins(sems[0], from_root)

    @pl.when(me != 0)
    def _():
        prepare_place(work[4])
        pltpu.make_async_remote_copy(
            src_ref=from_root,
            dst_ref=from_root,
            send_sem=sems[0].at[0],
            recv_sem=sems[0].at[1],
            device_id={"clique": 0},
            device_id_type=MESH,
        ).wait_recv()

    for k in range(4):
        arrived[0, k] = from_root[k]

    def prepare_1(c):
        out_1[c] = from_root[info[SOURCE + c] % 4]

    send_pieces(me, out_1, in_1, sems[1], prepare_1)
    in_1[me] = from_root[info[SOURCE + me] % 4]
    all_but_one(me, out_1, in_1, sems[1]).wait()

    @pl.when(me != 0)
    def _():
        drop = info[OWN_DROP]

        def body(piece, carry):
            value = in_1[piece] - message[piece]
            for k in range(4):
                held[piece, k] = jnp.where(drop == k, value, 0.0)
            return carry

        lax.fori_loop(0, PIECES, body, 0)
        place_slots(table, belief, held, work[3:], prepared=True)
        send_margins(sems[2], arrived.at[me])
        part_of(me, PIECES - 2, margins, arrived, sems[2]).wait_recv()

    @pl.when(me == 0)
    def _():
        part_of(me, PIECES - 1, margins, arrived, sems[2]).wait_recv()

    def prepare_2(c):
        out_2[c] = arrived[info[SOURCE + c] // 4, info[SOURCE + c] % 4]

    send_pieces(me, out_2, received, sems[3], prepare_2)
    received[me] = arrived[info[SOURCE + me] // 4, info[SOURCE + me] % 4]
    all_but_one(me, out_2, received, sems[3]).wait()

    @pl.when(me == 0)
    def _():
        part_of(me, PIECES - 1, margins, arrived, sems[0]).wait_send()

    @pl.when(me != 0)
    def _():
        part_of(me, PIECES - 1, margins, arrived, sems[2]).wait_send()

    @pl.when(sends)
    def _():
        copy.wait_send()


MESSAGE = jax.ShapeDtypeStruct((PIECES, 8, 128), F32)
SLOTS = jax.ShapeDtypeStruct((PIECES, 4, 8, 128), F32)
TABLE = jax.ShapeDtypeStruct((1024, 1024), F32)
ANY_SPEC = pl.BlockSpec(memory_space=pl.ANY)
S_SPEC = pl.BlockSpec(memory_space=SMEM)
V_SPEC = pl.BlockSpec(memory_space=VMEM)
HELD_MESSAGE = VMEM((PIECES, 8, 128), F32)
HELD_SUMS = VMEM((PIECES + 1, 8, 128), F32)
HELD_SLOTS = VMEM((PIECES, 4, 8, 128), F32)
HELD_PIECE = VMEM((4, 8, 128), F32)
HELD_TABLE = VMEM((1024, 1024), F32)
PLACE_TOOLS = [VMEM((256, 256), jnp.bfloat16), VMEM((256, 1024), jnp.bfloat16)]
WORK = [VMEM((1024, 128), F32), VMEM((1024, 128), F32), VMEM((8, 32, 128), F32)] + PLACE_TOOLS
PAIR_SEMS = pltpu.SemaphoreType.DMA((2,))


def call(kernel, name, ins, outs, out_specs, scratch, collective=None, limit=20):
    more = {} if collective is None else dict(collective_id=collective, has_side_effects=True)
    return pl.pallas_call(
        kernel,
        name=name,
        in_specs=ins,
        out_shape=outs,
        out_specs=out_specs,
        scratch_shapes=scratch,
        compiler_params=pltpu.CompilerParams(vmem_limit_bytes=limit * 2**20, **more),
    )


def per_device(potentials, parent, child_drop, parent_drop):
    table = potentials.reshape(1024, 1024)
    trees = jnp.concatenate([child_drop, parent_drop, parent])
    message, info = call(
        first_kernel,
        "first",
        [ANY_SPEC] * 2,
        (MESSAGE, jax.ShapeDtypeStruct((INFO,), jnp.int32)),
        (V_SPEC, S_SPEC),
        [HELD_TABLE, SMEM((9, 32), jnp.int32)]
        + WORK
        + [pltpu.SemaphoreType.DMA((CHUNKS,)), pltpu.SemaphoreType.DMA],
        limit=53,
    )(trees, table)
    slots = call(
        sums_kernel,
        "sums",
        [S_SPEC, V_SPEC],
        SLOTS,
        V_SPEC,
        [HELD_MESSAGE, HELD_SUMS, HELD_SLOTS, PAIR_SEMS, PAIR_SEMS],
        collective=0,
    )(info, message)
    message = call(
        up_kernel, "up", [S_SPEC] + [V_SPEC] * 2, MESSAGE, V_SPEC, [HELD_TABLE] + WORK
    )(info, table, slots)
    slots = call(
        root_sums_kernel,
        "root_sums",
        [S_SPEC] + [V_SPEC] * 2,
        SLOTS,
        V_SPEC,
        [HELD_MESSAGE, HELD_SUMS, HELD_PIECE, PAIR_SEMS, PAIR_SEMS],
        collective=1,
    )(info, message, slots)

    def hop(step, sent):
        return call(
            functools.partial(hop_kernel, step),
            f"hop_{step}",
            [V_SPEC],
            MESSAGE,
            V_SPEC,
            [PAIR_SEMS],
            collective=2 + step,
        )(sent)

    sent, table = call(
        chain_first_kernel, "chain_1", [S_SPEC] + [V_SPEC] * 2, (MESSAGE, TABLE), (V_SPEC, V_SPEC), WORK
    )(info, table, slots)
    first = hop(1, sent)
    sent = call(
        functools.partial(chain_kernel, 2),
        "chain_2",
        [S_SPEC] + [V_SPEC] * 2,
        MESSAGE,
        V_SPEC,
        [HELD_TABLE] + WORK,
    )(info, table, first)
    second = hop(2, sent)
    sent, table = call(
        functools.partial(chain_kernel, 3),
        "chain_3",
        [S_SPEC] + [V_SPEC] * 2,
        (MESSAGE, TABLE),
        (V_SPEC, V_SPEC),
        WORK,
    )(info, table, second)
    received, last_root = call(
        down_kernel,
        "down",
        [S_SPEC] + [V_SPEC] * 4,
        (MESSAGE, MESSAGE),
        (V_SPEC, V_SPEC),
        [HELD_TABLE] + [HELD_SLOTS] * 3 + [HELD_PIECE] + [HELD_MESSAGE] * 4 + WORK + [PAIR_SEMS] * 5,
        collective=2,
    )(info, table, first, sent, message)
    out = call(
        final_kernel,
        "final",
        [S_SPEC] + [V_SPEC] * 4,
        TABLE,
        ANY_SPEC,
        [HELD_TABLE, HELD_MESSAGE] + PLACE_TOOLS + [pltpu.SemaphoreType.DMA((4,))],
    )(info, table, last_root, received, message)
    return out.reshape(1, 1, 1024, 1024)


def solution(mesh):
    specs = (P("subtree", "clique", None, None), P("subtree", None), P(), P())
    return jax.shard_map(
        per_device,
        mesh=mesh,
        in_specs=specs,
        out_specs=P("subtree", "clique", None, None),
        check_vma=False,
    )
```

```python
import functools

import jax
import jax.numpy as jnp
from jax import lax
from jax.experimental import pallas as pl
from jax.experimental.pallas import tpu as pltpu
from jax.sharding import PartitionSpec as P

PIECES = 32
CHUNKS = 8
MESH = pl.DeviceIdType.MESH
F32 = jnp.float32
VMEM = pltpu.VMEM
SMEM = pltpu.SMEM


def lanes():
    return lax.broadcasted_iota(jnp.int32, (8, 128), 1)


def rows():
    return lax.broadcasted_iota(jnp.int32, (8, 128), 0)


def take(vec, index):
    return jnp.take_along_axis(vec, index, axis=1, mode="promise_in_bounds")


def tree(parts, op):
    parts = list(parts)
    while len(parts) > 1:
        parts = [op(*parts[n : n + 2]) if n + 1 < len(parts) else parts[n] for n in range(0, len(parts), 2)]
    return parts[0]


def tile(table, a0, i, t):
    return table[pl.ds(pl.multiple_of(a0 * 32 + 8 * i, 8), 8), 128 * t : 128 * (t + 1)]


def prepare_place(hot):
    row = lax.broadcasted_iota(jnp.int32, (256, 1024), 0)
    column = lax.broadcasted_iota(jnp.int32, (256, 1024), 1)
    level = jnp.where(row < 128, column // 32, column % 32)
    hot[...] = jnp.where((level == row % 32) & (row % 128 < 96), 1.0, 0.0).astype(jnp.bfloat16)


def three_parts(vec):
    high = vec.astype(jnp.bfloat16).astype(F32)
    rest = vec - high
    middle = rest.astype(jnp.bfloat16).astype(F32)
    group = lanes() // 32
    return jnp.where(group == 0, high, jnp.where(group == 1, middle, jnp.where(group == 2, rest - middle, 0.0)))


def place(source, target, terms, tools, after=None):
    left, hot = tools
    lane, row = lanes(), rows()
    spread = (row % 4) * 32 + lane % 32
    by_matrix = [k for k in (3, 2) if k in terms] if 3 in terms else []
    depth = 128 * len(by_matrix)

    def body(part, carry):
        def levels(k, s, i):
            read = terms[k][1]
            return take(jnp.where(row < 4, read(part * 8 + 2 * i, s), read(part * 8 + 2 * i + 1, s)), spread)

        if by_matrix:
            for s in range(8):
                for half in range(2):
                    both = [
                        jnp.concatenate([three_parts(levels(k, s, i)) for k in by_matrix], axis=1)
                        for i in (2 * half, 2 * half + 1)
                    ]
                    at = 32 * s + 16 * half
                    left[at : at + 16, :depth] = jnp.concatenate(both, axis=0).astype(jnp.bfloat16)
        for n in range(4):
            if by_matrix:
                back = jnp.dot(
                    left[:, :depth], hot[:depth, 256 * n : 256 * (n + 1)], preferred_element_type=F32
                )
            for s in range(8):
                a0 = part * 8 + s
                third = [levels(2, s, i) for i in range(4)] if 2 in terms and not by_matrix else None
                for t in (2 * n, 2 * n + 1):
                    second = terms[1][1](part * 8 + t, s) if 1 in terms else None
                    for i in range(4):
                        adds = []
                        if 0 in terms:
                            adds.append(terms[0][0](i * 8 + t))
                        if 1 in terms:
                            adds.append(jnp.broadcast_to(second, (8, 128)))
                        if third is not None:
                            adds.append(third[i])
                        if by_matrix:
                            at, column = 32 * s + 8 * i, 128 * (t - 2 * n)
                            adds.append(back[at : at + 8, column : column + 128])
                        where = pl.ds(pl.multiple_of(a0 * 32 + 8 * i, 8), 8)
                        value = tile(source, a0, i, t) + functools.reduce(jnp.add, adds)
                        target[where, 128 * t : 128 * (t + 1)] = value
        if after is not None:
            after(part)
        return carry

    lax.fori_loop(0, 4, body, 0)


def place_slots(source, target, slots, tools, after=None):
    def readers(k):
        return lambda piece: slots[piece, k], lambda piece, s: slots[piece, k, pl.ds(s, 1), :]

    place(source, target, {k: readers(k) for k in range(4)}, tools, after)


def place_message(source, target, message, axis, tools, after=None):
    for k in range(4):

        @pl.when(axis == k)
        def _(k=k):
            readers = (lambda piece: message[piece], lambda piece, s: message[piece, pl.ds(s, 1), :])
            place(source, target, {k: readers}, tools, after)


def pick(parts):
    group = lanes() // 32
    return jnp.where(
        group == 0, parts[0], jnp.where(group == 1, parts[1], jnp.where(group == 2, parts[2], parts[3]))
    )


def margin_0(table, put, work, before=None):
    if before is not None:
        for n in range(CHUNKS):
            before(n)

    def body(i, carry):
        for t in range(8):
            parts = [tile(table, a0, i, t) for a0 in range(32)]
            top = tree(parts, jnp.maximum)
            total = tree([jnp.exp(part - top) for part in parts], jnp.add)
            put(i * 8 + t, 1, None, top + jnp.log(total))
        return carry

    lax.fori_loop(0, 4, body, 0)


def over_rows(vec, op):
    for shift in (4, 2, 1):
        vec = op(vec, pltpu.roll(vec, shift, 0))
    return vec


def by_blocks(body, before):
    def block(n, carry):
        if before is not None:
            before(n)
        for a0 in range(4):
            body(n * 4 + a0, carry)
        return carry

    lax.fori_loop(0, 8, block, 0)


def margin_1(table, put, work, before=None):
    def body(a0, carry):
        for t in range(8):
            parts = [tile(table, a0, i, t) for i in range(4)]
            top = over_rows(tree(parts, jnp.maximum), jnp.maximum)
            total = over_rows(tree([jnp.exp(part - top) for part in parts], jnp.add), jnp.add)
            put((a0 // 8) * 8 + t, 1, a0 % 8, (top + jnp.log(total))[0:1])
        return carry

    by_blocks(body, before)


def put_turned(across, flat, put):
    for block in range(8):
        part = across[block]
        flat[128 * block : 128 * (block + 1), :] = jnp.concatenate([part] * 4, axis=0).T
    for a0 in range(32):
        put((a0 // 8) * 8, 8, a0 % 8, pick([flat[pl.ds(a0 * 32 + q, 8, stride=4), :] for q in range(4)]))


def turned_margins(table, put_2, put_3, work, before=None):
    flat, across_2, across_3, kept = work[:4]

    def body(block, carry):
        if before is not None:
            before(block)
        tops = None
        for t in range(8):
            turned = table[pl.ds(pl.multiple_of(block * 128, 128), 128), 128 * t : 128 * (t + 1)].T
            tiles = [[turned[32 * g + 8 * m : 32 * g + 8 * (m + 1)] for m in range(4)] for g in range(4)]
            if put_3 is not None:
                for g in range(4):
                    top = over_rows(tree(tiles[g], jnp.maximum), jnp.maximum)
                    total = over_rows(tree([jnp.exp(part - top) for part in tiles[g]], jnp.add), jnp.add)
                    across_3[block, 4 * t + g : 4 * t + g + 1, :] = (top + jnp.log(total))[0:1]
            if put_2 is not None:
                kept[block, t] = turned
                here = [tree([tiles[g][m] for g in range(4)], jnp.maximum) for m in range(4)]
                tops = here if tops is None else [jnp.maximum(a, b) for a, b in zip(tops, here)]
        if put_2 is not None:
            totals = None
            for t in range(8):
                here = [
                    tree(
                        [jnp.exp(kept[block, t, 32 * g + 8 * m : 32 * g + 8 * (m + 1), :] - tops[m]) for g in range(4)],
                        jnp.add,
                    )
                    for m in range(4)
                ]
                totals = here if totals is None else [a + b for a, b in zip(totals, here)]
            for m in range(4):
                across_2[block, 8 * m : 8 * (m + 1), :] = tops[m] + jnp.log(totals[m])
        return carry

    lax.fori_loop(0, 8, body, 0, unroll=4)
    if put_2 is not None:
        put_turned(across_2, flat, put_2)
    if put_3 is not None:
        put_turned(across_3, flat, put_3)


def margin_2(table, put, work, before=None):
    turned_margins(table, put, None, work, before)


def margin_3(table, put, work, before=None):
    turned_margins(table, None, put, work, before)


MARGINS = (margin_0, margin_1, margin_2, margin_3)


def message_put(message):
    def put(piece, count, row, value):
        if row is None:
            message[piece] = value
        elif count == 1:
            message[piece, pl.ds(row, 1), :] = value
        else:
            message[pl.ds(piece, count), row, :] = value

    return put


def slot_put(slots, k):
    def put(piece, count, row, value):
        if row is None:
            slots[piece, k] = value
        elif count == 1:
            slots[piece, k, pl.ds(row, 1), :] = value
        else:
            slots[pl.ds(piece, count), k, row, :] = value

    return put


def chosen_margin(table, axis, message, work, before=None):
    for k in range(4):

        @pl.when(axis == k)
        def _(k=k):
            MARGINS[k](table, message_put(message), work, before)


def copy_slots(source, target):
    def body(piece, carry):
        for k in range(4):
            target[piece, k] = source[piece, k]
        return carry

    lax.fori_loop(0, PIECES, body, 0)


PREVIOUS, LAST, SOURCE, OWN_DROP, CHAIN_AXIS, CHAIN_SLOT, INFO = 0, 32, 160, 192, 192, 196, 256


def first_kernel(trees_in, potentials, message, info, hot, table, trees, *rest):
    work, load_sems, sems = rest[:4], rest[4], rest[5]
    me, s = lax.axis_index("clique"), lax.axis_index("subtree")
    size = 1024 // CHUNKS

    def load(n):
        at = pl.ds(pl.multiple_of(size * n, size), size)
        return pltpu.make_async_copy(potentials.at[at], table.at[at], load_sems.at[n])

    small = pltpu.make_async_copy(trees_in, trees, sems)
    small.start()
    for n in range(CHUNKS):
        load(n).start()
    prepare_place(hot)
    for n in range(128):
        info[LAST + n] = PIECES
    small.wait()
    info[PREVIOUS] = PIECES
    info[SOURCE] = trees[4 + s, 0]

    def link(c, carry):
        target = trees[8, c] * 4 + trees[4 + s, c]
        info[SOURCE + c] = target
        info[PREVIOUS + c] = info[LAST + target]
        info[LAST + target] = c
        return carry

    lax.fori_loop(1, PIECES, link, 0)
    own = trees[s, me]
    info[OWN_DROP] = own
    to_next = trees[4 + jnp.minimum(s + 1, 3), 0]
    to_previous = trees[s, 0]
    for step, sender, receiver in ((1, 0, 2), (2, 1, 1), (3, 2, 0)):
        active = (me == 0) & (((s == 1) | (s == 2)) == (step > 1))
        info[CHAIN_AXIS + step] = jnp.where(active, jnp.where(s == sender, to_next, to_previous), 4)
        info[CHAIN_SLOT + step] = jnp.where(s == receiver, to_next, to_previous)
    chosen_margin(table, own, message, work, lambda n: load(n).wait())


def up_kernel(info, hot, table, slots, message, placed, *work):
    place_slots(table, placed, slots, (work[4], hot))
    chosen_margin(placed, info[OWN_DROP], message, work)


def chain_first_kernel(info, hot, table, slots, message, placed, *work):
    place_slots(table, placed, slots, (work[4], hot))
    chosen_margin(placed, info[CHAIN_AXIS + 1], message, work)


def chain_kernel(step, info, hot, table, arrived, message, placed, *work):
    place_message(table, placed, arrived, info[CHAIN_SLOT + step - 1], (work[4], hot))
    chosen_margin(placed, info[CHAIN_AXIS + step], message, work)


def inner_root(s):
    return (s == 1) | (s == 2)


def last_root_slot(info):
    inner = inner_root(lax.axis_index("subtree"))
    return jnp.where(inner, info[CHAIN_SLOT + 1], info[CHAIN_SLOT + 3])


def final_kernel(info, hot, table, last_root, received, message, out, belief, held, left, sems):
    below = lax.axis_index("clique") != 0
    top = jnp.max(tree([received[piece] for piece in range(PIECES)], jnp.maximum))
    total = tree([jnp.exp(received[piece] - top) for piece in range(PIECES)], jnp.add)
    log_total = top + jnp.log(jnp.broadcast_to(jnp.sum(total), (8, 128)))
    for piece in range(PIECES):
        held[piece] = jnp.where(below, received[piece] - message[piece], last_root[piece]) - log_total

    def out_copy(part):
        at = pl.ds(pl.multiple_of(part * 256, 256), 256)
        return pltpu.make_async_copy(belief.at[at], out.at[at], sems.at[part])

    axis = jnp.where(below, info[OWN_DROP], last_root_slot(info))
    place_message(table, belief, held, axis, (left, hot), after=lambda part: out_copy(part).start())
    for part in range(4):
        out_copy(part).wait()


TURNS = sorted(
    (turn for turn in range(1, PIECES)),
    key=lambda turn: -(min(turn // 8, 4 - turn // 8) + min(turn // 2 % 4, 4 - turn // 2 % 4)),
)


def turned(me, turn):
    y, z, core = (me // 8 + turn // 8) % 4, (me // 2 % 4 + turn // 2 % 4) % 4, (me % 2 + turn % 2) % 2
    return y * 8 + z * 2 + core


def announce(me):
    barrier = pltpu.get_barrier_semaphore()
    for turn in TURNS:
        pl.semaphore_signal(barrier, inc=1, device_id={"clique": turned(me, turn)}, device_id_type=MESH)


def await_others():
    pl.semaphore_wait(pltpu.get_barrier_semaphore(), PIECES - 1)


def enter(me):
    announce(me)
    await_others()


def send_pieces(me, source, target, sems, prepare=None):
    for turn in TURNS:
        other = turned(me, turn)
        if prepare is not None:
            prepare(other)
        pltpu.make_async_remote_copy(
            src_ref=source.at[other],
            dst_ref=target.at[me],
            send_sem=sems.at[0],
            recv_sem=sems.at[1],
            device_id={"clique": other},
            device_id_type=MESH,
        ).start()


def part_of(me, count, source, target, sems):
    return pltpu.make_async_remote_copy(
        src_ref=source.at[pl.ds(0, count)],
        dst_ref=target.at[pl.ds(0, count)],
        send_sem=sems.at[0],
        recv_sem=sems.at[1],
        device_id={"clique": (me + 1) % PIECES},
        device_id_type=MESH,
    )


def all_but_one(me, source, target, sems):
    return part_of(me, PIECES - 1, source, target, sems)


def gather_up(me, info, message, arrived, sums, sems):
    enter(me)
    send_pieces(me, message, arrived, sems)
    arrived[me] = message[me]
    sums[PIECES] = jnp.zeros((8, 128), F32)
    all_but_one(me, message, arrived, sems).wait_recv()
    for c in range(1, PIECES):
        sums[c] = arrived[c] + sums[info[PREVIOUS + c]]
    all_but_one(me, message, arrived, sems).wait_send()


def sums_kernel(info, message, slots, arrived, sums, outgoing, sems, more_sems):
    me = lax.axis_index("clique")
    gather_up(me, info, message, arrived, sums, sems)

    def prepare(p):
        for k in range(4):
            outgoing[p, k] = sums[info[LAST + p * 4 + k]]

    send_pieces(me, outgoing, slots, more_sems, prepare)
    for k in range(4):
        slots[me, k] = sums[info[LAST + me * 4 + k]]
    all_but_one(me, outgoing, slots, more_sems).wait()


def root_sums_kernel(info, message, old_slots, slots, arrived, sums, outgoing, sems, more_sems):
    me = lax.axis_index("clique")
    gather_up(me, info, message, arrived, sums, sems)

    @pl.when(me != 0)
    def _():
        for k in range(4):
            outgoing[k] = sums[info[LAST + k]]
        copy = pltpu.make_async_remote_copy(
            src_ref=outgoing,
            dst_ref=slots.at[me],
            send_sem=more_sems.at[0],
            recv_sem=more_sems.at[1],
            device_id={"clique": 0},
            device_id_type=MESH,
        )
        copy.start()
        copy_slots(old_slots, slots)
        copy.wait_send()

    @pl.when(me == 0)
    def _():
        for k in range(4):
            slots[0, k] = sums[info[LAST + k]]
        all_but_one(me, slots, slots, more_sems).wait_recv()


def to_root(s, step, source, target, sems):
    partner = 3 - s if step == 2 else s + 1 - 2 * (s % 2)
    return partner, pltpu.make_async_remote_copy(
        src_ref=source,
        dst_ref=target,
        send_sem=sems.at[0],
        recv_sem=sems.at[1],
        device_id={"subtree": partner},
        device_id_type=MESH,
    )


def hop_kernel(step, sent, arrived, sems):
    me, s = lax.axis_index("clique"), lax.axis_index("subtree")
    partner, copy = to_root(s, step, sent, arrived, sems)
    barrier = pltpu.get_barrier_semaphore()
    receives = (me == 0) & inner_root(s)
    sends = (me == 0) & (inner_root(s) == (step == 2))

    @pl.when(receives)
    def _():
        pl.semaphore_signal(barrier, inc=1, device_id={"subtree": partner}, device_id_type=MESH)

    @pl.when(sends)
    def _():
        pl.semaphore_wait(barrier, 1)
        copy.start()

    @pl.when(jnp.logical_not(receives))
    def _():
        for piece in range(PIECES):
            arrived[piece] = jnp.zeros((8, 128), F32)

    @pl.when(receives)
    def _():
        copy.wait_recv()

    @pl.when(sends)
    def _():
        copy.wait_send()


def send_slots(me, start, source, target, sems):
    for turn in TURNS:
        other = turned(me, turn)
        pltpu.make_async_remote_copy(
            src_ref=source.at[other, pl.ds(start, 1)],
            dst_ref=target,
            send_sem=sems.at[0],
            recv_sem=sems.at[1],
            device_id={"clique": other},
            device_id_type=MESH,
        ).start()


def down_kernel(info, hot, table, first, sent, message, received, last_root, *scratch):
    belief, margins, held, arrived, from_root, third, out_1, in_1, out_2 = scratch[:9]
    work, sems = scratch[9:14], scratch[14:]
    tools = (work[4], hot)
    me, s = lax.axis_index("clique"), lax.axis_index("subtree")
    inner = inner_root(s)
    sends, receives = (me == 0) & inner, (me == 0) & jnp.logical_not(inner)
    partner, copy = to_root(s, 3, sent, third, sems[4])
    barrier = pltpu.get_barrier_semaphore()

    @pl.when(receives)
    def _():
        pl.semaphore_signal(barrier, inc=1, device_id={"subtree": partner}, device_id_type=MESH)

    announce(me)

    @pl.when(sends)
    def _():
        pl.semaphore_wait(barrier, PIECES)
        copy.start()

    @pl.when(jnp.logical_not(sends))
    def _():
        pl.semaphore_wait(barrier, PIECES - 1)

    def send_margins(pair, target, order):
        for group in order:
            if len(group) == 2:
                turned_margins(belief, slot_put(margins, 2), slot_put(margins, 3), work)
            else:
                MARGINS[group[0]](belief, slot_put(margins, group[0]), work)
            for k in group:
                send_slots(me, k, margins, target.at[pl.ds(k, 1)], pair)
        for k in range(4):
            target[k] = margins[me, k]

    @pl.when(receives)
    def _():
        copy.wait_recv()

        def body(piece, carry):
            last_root[piece] = third[piece]
            return carry

        lax.fori_loop(0, PIECES, body, 0)

    @pl.when(jnp.logical_not(receives))
    def _():
        def body(piece, carry):
            last_root[piece] = first[piece]
            return carry

        lax.fori_loop(0, PIECES, body, 0)

    @pl.when(me == 0)
    def _():
        slot = last_root_slot(info)

        def body(piece, carry):
            for k in range(4):
                held[piece, k] = jnp.where(slot == k, last_root[piece], 0.0)
            return carry

        lax.fori_loop(0, PIECES, body, 0)
        place_slots(table, belief, held, tools)
        send_margins(sems[0], from_root, ((2, 3), (1,), (0,)))

    @pl.when(me != 0)
    def _():
        pltpu.make_async_remote_copy(
            src_ref=from_root,
            dst_ref=from_root,
            send_sem=sems[0].at[0],
            recv_sem=sems[0].at[1],
            device_id={"clique": 0},
            device_id_type=MESH,
        ).wait_recv()

    for k in range(4):
        arrived[0, k] = from_root[k]

    def prepare_1(c):
        out_1[c] = from_root[info[SOURCE + c] % 4]

    send_pieces(me, out_1, in_1, sems[1], prepare_1)
    in_1[me] = from_root[info[SOURCE + me] % 4]
    all_but_one(me, out_1, in_1, sems[1]).wait()

    @pl.when(me != 0)
    def _():
        drop = info[OWN_DROP]

        def body(piece, carry):
            value = in_1[piece] - message[piece]
            for k in range(4):
                held[piece, k] = jnp.where(drop == k, value, 0.0)
            return carry

        lax.fori_loop(0, PIECES, body, 0)
        place_slots(table, belief, held, tools)
        send_margins(sems[2], arrived.at[me], ((0,), (1,), (2, 3)))
        part_of(me, PIECES - 2, margins, arrived, sems[2]).wait_recv()

    @pl.when(me == 0)
    def _():
        part_of(me, PIECES - 1, margins, arrived, sems[2]).wait_recv()

    def prepare_2(c):
        out_2[c] = arrived[info[SOURCE + c] // 4, info[SOURCE + c] % 4]

    send_pieces(me, out_2, received, sems[3], prepare_2)
    received[me] = arrived[info[SOURCE + me] // 4, info[SOURCE + me] % 4]
    all_but_one(me, out_2, received, sems[3]).wait()

    @pl.when(me == 0)
    def _():
        part_of(me, PIECES - 1, margins, arrived, sems[0]).wait_send()

    @pl.when(me != 0)
    def _():
        part_of(me, PIECES - 1, margins, arrived, sems[2]).wait_send()

    @pl.when(sends)
    def _():
        copy.wait_send()


MESSAGE = jax.ShapeDtypeStruct((PIECES, 8, 128), F32)
SLOTS = jax.ShapeDtypeStruct((PIECES, 4, 8, 128), F32)
TABLE = jax.ShapeDtypeStruct((1024, 1024), F32)
ANY_SPEC = pl.BlockSpec(memory_space=pl.ANY)
S_SPEC = pl.BlockSpec(memory_space=SMEM)
V_SPEC = pl.BlockSpec(memory_space=VMEM)
HELD_MESSAGE = VMEM((PIECES, 8, 128), F32)
HELD_SUMS = VMEM((PIECES + 1, 8, 128), F32)
HELD_SLOTS = VMEM((PIECES, 4, 8, 128), F32)
HELD_PIECE = VMEM((4, 8, 128), F32)
HELD_TABLE = VMEM((1024, 1024), F32)
LEFT = VMEM((256, 256), jnp.bfloat16)
HOT = jax.ShapeDtypeStruct((256, 1024), jnp.bfloat16)
WORK = [VMEM((1024, 128), F32), VMEM((8, 32, 128), F32), VMEM((8, 32, 128), F32), VMEM((8, 8, 128, 128), F32), LEFT]
PAIR_SEMS = pltpu.SemaphoreType.DMA((2,))


def call(kernel, name, ins, outs, out_specs, scratch, collective=None, limit=20):
    more = {} if collective is None else dict(collective_id=collective, has_side_effects=True)
    return pl.pallas_call(
        kernel,
        name=name,
        in_specs=ins,
        out_shape=outs,
        out_specs=out_specs,
        scratch_shapes=scratch,
        compiler_params=pltpu.CompilerParams(vmem_limit_bytes=limit * 2**20, **more),
    )


def per_device(potentials, parent, child_drop, parent_drop):
    table = potentials.reshape(1024, 1024)
    trees = jnp.concatenate([child_drop, parent_drop, parent])
    message, info, hot = call(
        first_kernel,
        "first",
        [ANY_SPEC] * 2,
        (MESSAGE, jax.ShapeDtypeStruct((INFO,), jnp.int32), HOT),
        (V_SPEC, S_SPEC, V_SPEC),
        [HELD_TABLE, SMEM((9, 32), jnp.int32)]
        + WORK[:4]
        + [pltpu.SemaphoreType.DMA((CHUNKS,)), pltpu.SemaphoreType.DMA],
        limit=53,
    )(trees, table)
    slots = call(
        sums_kernel,
        "sums",
        [S_SPEC, V_SPEC],
        SLOTS,
        V_SPEC,
        [HELD_MESSAGE, HELD_SUMS, HELD_SLOTS, PAIR_SEMS, PAIR_SEMS],
        collective=0,
    )(info, message)
    message = call(
        up_kernel, "up", [S_SPEC] + [V_SPEC] * 3, MESSAGE, V_SPEC, [HELD_TABLE] + WORK
    )(info, hot, table, slots)
    slots = call(
        root_sums_kernel,
        "root_sums",
        [S_SPEC] + [V_SPEC] * 2,
        SLOTS,
        V_SPEC,
        [HELD_MESSAGE, HELD_SUMS, HELD_PIECE, PAIR_SEMS, PAIR_SEMS],
        collective=1,
    )(info, message, slots)

    def hop(step, sent):
        return call(
            functools.partial(hop_kernel, step),
            f"hop_{step}",
            [V_SPEC],
            MESSAGE,
            V_SPEC,
            [PAIR_SEMS],
            collective=2 + step,
        )(sent)

    sent, table = call(
        chain_first_kernel, "chain_1", [S_SPEC] + [V_SPEC] * 3, (MESSAGE, TABLE), (V_SPEC, V_SPEC), WORK
    )(info, hot, table, slots)
    first = hop(1, sent)
    sent = call(
        functools.partial(chain_kernel, 2),
        "chain_2",
        [S_SPEC] + [V_SPEC] * 3,
        MESSAGE,
        V_SPEC,
        [HELD_TABLE] + WORK,
    )(info, hot, table, first)
    second = hop(2, sent)
    sent, table = call(
        functools.partial(chain_kernel, 3),
        "chain_3",
        [S_SPEC] + [V_SPEC] * 3,
        (MESSAGE, TABLE),
        (V_SPEC, V_SPEC),
        WORK,
    )(info, hot, table, second)
    received, last_root = call(
        down_kernel,
        "down",
        [S_SPEC] + [V_SPEC] * 5,
        (MESSAGE, MESSAGE),
        (V_SPEC, V_SPEC),
        [HELD_TABLE] + [HELD_SLOTS] * 3 + [HELD_PIECE] + [HELD_MESSAGE] * 4 + WORK + [PAIR_SEMS] * 5,
        collective=2,
    )(info, hot, table, first, sent, message)
    out = call(
        final_kernel,
        "final",
        [S_SPEC] + [V_SPEC] * 5,
        TABLE,
        ANY_SPEC,
        [HELD_TABLE, HELD_MESSAGE, LEFT, pltpu.SemaphoreType.DMA((4,))],
    )(info, hot, table, last_root, received, message)
    return out.reshape(1, 1, 1024, 1024)


def solution(mesh):
    specs = (P("subtree", "clique", None, None), P("subtree", None), P(), P())
    return jax.shard_map(
        per_device,
        mesh=mesh,
        in_specs=specs,
        out_specs=P("subtree", "clique", None, None),
        check_vma=False,
    )
```

```python
import functools

import jax
import jax.numpy as jnp
from jax import lax
from jax.experimental import pallas as pl
from jax.experimental.pallas import tpu as pltpu
from jax.sharding import PartitionSpec as P

PIECES = 32
CHUNKS = 8
MESH = pl.DeviceIdType.MESH
F32 = jnp.float32
VMEM = pltpu.VMEM
SMEM = pltpu.SMEM


def lanes():
    return lax.broadcasted_iota(jnp.int32, (8, 128), 1)


def rows():
    return lax.broadcasted_iota(jnp.int32, (8, 128), 0)


def take(vec, index):
    return jnp.take_along_axis(vec, index, axis=1, mode="promise_in_bounds")


def tree(parts, op):
    parts = list(parts)
    while len(parts) > 1:
        parts = [op(*parts[n : n + 2]) if n + 1 < len(parts) else parts[n] for n in range(0, len(parts), 2)]
    return parts[0]


def tile(table, a0, i, t):
    return table[pl.ds(pl.multiple_of(a0 * 32 + 8 * i, 8), 8), 128 * t : 128 * (t + 1)]


def prepare_place(hot):
    row = lax.broadcasted_iota(jnp.int32, (256, 1024), 0)
    column = lax.broadcasted_iota(jnp.int32, (256, 1024), 1)
    level = jnp.where(row < 128, column // 32, column % 32)
    hot[...] = jnp.where((level == row % 32) & (row % 128 < 96), 1.0, 0.0).astype(jnp.bfloat16)


def three_parts(vec):
    high = vec.astype(jnp.bfloat16).astype(F32)
    rest = vec - high
    middle = rest.astype(jnp.bfloat16).astype(F32)
    group = lanes() // 32
    return jnp.where(group == 0, high, jnp.where(group == 1, middle, jnp.where(group == 2, rest - middle, 0.0)))


def place(source, target, terms, tools, after=None):
    left, hot = tools
    lane, row = lanes(), rows()
    spread = (row % 4) * 32 + lane % 32
    by_matrix = [k for k in (3, 2) if k in terms] if 3 in terms else []
    depth = 128 * len(by_matrix)

    def body(part, carry):
        def levels(k, s, i):
            read = terms[k][1]
            return take(jnp.where(row < 4, read(part * 8 + 2 * i, s), read(part * 8 + 2 * i + 1, s)), spread)

        if by_matrix:
            for s in range(8):
                for half in range(2):
                    both = [
                        jnp.concatenate([three_parts(levels(k, s, i)) for k in by_matrix], axis=1)
                        for i in (2 * half, 2 * half + 1)
                    ]
                    at = 32 * s + 16 * half
                    left[at : at + 16, :depth] = jnp.concatenate(both, axis=0).astype(jnp.bfloat16)
        for n in range(4):
            if by_matrix:
                back = jnp.dot(
                    left[:, :depth], hot[:depth, 256 * n : 256 * (n + 1)], preferred_element_type=F32
                )
            for s in range(8):
                a0 = part * 8 + s
                third = [levels(2, s, i) for i in range(4)] if 2 in terms and not by_matrix else None
                for t in (2 * n, 2 * n + 1):
                    second = terms[1][1](part * 8 + t, s) if 1 in terms else None
                    for i in range(4):
                        adds = []
                        if 0 in terms:
                            adds.append(terms[0][0](i * 8 + t))
                        if 1 in terms:
                            adds.append(jnp.broadcast_to(second, (8, 128)))
                        if third is not None:
                            adds.append(third[i])
                        if by_matrix:
                            at, column = 32 * s + 8 * i, 128 * (t - 2 * n)
                            adds.append(back[at : at + 8, column : column + 128])
                        where = pl.ds(pl.multiple_of(a0 * 32 + 8 * i, 8), 8)
                        value = tile(source, a0, i, t) + functools.reduce(jnp.add, adds)
                        target[where, 128 * t : 128 * (t + 1)] = value
        if after is not None:
            after(part)
        return carry

    lax.fori_loop(0, 4, body, 0)


def place_slots(source, target, slots, tools, after=None):
    def readers(k):
        return lambda piece: slots[piece, k], lambda piece, s: slots[piece, k, pl.ds(s, 1), :]

    place(source, target, {k: readers(k) for k in range(4)}, tools, after)


def place_message(source, target, message, axis, tools, after=None):
    for k in range(4):

        @pl.when(axis == k)
        def _(k=k):
            readers = (lambda piece: message[piece], lambda piece, s: message[piece, pl.ds(s, 1), :])
            place(source, target, {k: readers}, tools, after)


def pick(parts):
    group = lanes() // 32
    return jnp.where(
        group == 0, parts[0], jnp.where(group == 1, parts[1], jnp.where(group == 2, parts[2], parts[3]))
    )


def margin_0(table, put, work, before=None):
    if before is not None:
        for n in range(CHUNKS):
            before(n)

    def body(i, carry):
        for t in range(8):
            parts = [tile(table, a0, i, t) for a0 in range(32)]
            top = tree(parts, jnp.maximum)
            total = tree([jnp.exp(part - top) for part in parts], jnp.add)
            put(i * 8 + t, 1, None, top + jnp.log(total))
        return carry

    lax.fori_loop(0, 4, body, 0)


def over_rows(vec, op):
    for shift in (4, 2, 1):
        vec = op(vec, pltpu.roll(vec, shift, 0))
    return vec


def by_blocks(body, before):
    def block(n, carry):
        if before is not None:
            before(n)
        for a0 in range(4):
            body(n * 4 + a0, carry)
        return carry

    lax.fori_loop(0, 8, block, 0)


def margin_1(table, put, work, before=None):
    def body(a0, carry):
        for t in range(8):
            parts = [tile(table, a0, i, t) for i in range(4)]
            top = over_rows(tree(parts, jnp.maximum), jnp.maximum)
            total = over_rows(tree([jnp.exp(part - top) for part in parts], jnp.add), jnp.add)
            put((a0 // 8) * 8 + t, 1, a0 % 8, (top + jnp.log(total))[0:1])
        return carry

    by_blocks(body, before)


def put_turned(across, flat, put):
    for block in range(8):
        part = across[block]
        flat[128 * block : 128 * (block + 1), :] = jnp.concatenate([part] * 4, axis=0).T
    for a0 in range(32):
        put((a0 // 8) * 8, 8, a0 % 8, pick([flat[pl.ds(a0 * 32 + q, 8, stride=4), :] for q in range(4)]))


def turned_margins(table, put_2, put_3, work, before=None):
    flat, across_2, across_3, kept = work[:4]

    def body(block, carry):
        if before is not None:
            before(block)
        tops = None
        for t in range(8):
            turned = table[pl.ds(pl.multiple_of(block * 128, 128), 128), 128 * t : 128 * (t + 1)].T
            tiles = [[turned[32 * g + 8 * m : 32 * g + 8 * (m + 1)] for m in range(4)] for g in range(4)]
            if put_3 is not None:
                for g in range(4):
                    top = over_rows(tree(tiles[g], jnp.maximum), jnp.maximum)
                    total = over_rows(tree([jnp.exp(part - top) for part in tiles[g]], jnp.add), jnp.add)
                    across_3[block, 4 * t + g : 4 * t + g + 1, :] = (top + jnp.log(total))[0:1]
            if put_2 is not None:
                kept[block, t] = turned
                here = [tree([tiles[g][m] for g in range(4)], jnp.maximum) for m in range(4)]
                tops = here if tops is None else [jnp.maximum(a, b) for a, b in zip(tops, here)]
        if put_2 is not None:
            totals = None
            for t in range(8):
                here = [
                    tree(
                        [jnp.exp(kept[block, t, 32 * g + 8 * m : 32 * g + 8 * (m + 1), :] - tops[m]) for g in range(4)],
                        jnp.add,
                    )
                    for m in range(4)
                ]
                totals = here if totals is None else [a + b for a, b in zip(totals, here)]
            for m in range(4):
                across_2[block, 8 * m : 8 * (m + 1), :] = tops[m] + jnp.log(totals[m])
        return carry

    lax.fori_loop(0, 8, body, 0, unroll=4)
    if put_2 is not None:
        put_turned(across_2, flat, put_2)
    if put_3 is not None:
        put_turned(across_3, flat, put_3)


def margin_2(table, put, work, before=None):
    turned_margins(table, put, None, work, before)


def margin_3(table, put, work, before=None):
    turned_margins(table, None, put, work, before)


MARGINS = (margin_0, margin_1, margin_2, margin_3)


def message_put(message):
    def put(piece, count, row, value):
        if row is None:
            message[piece] = value
        elif count == 1:
            message[piece, pl.ds(row, 1), :] = value
        else:
            message[pl.ds(piece, count), row, :] = value

    return put


def slot_put(slots, k):
    def put(piece, count, row, value):
        if row is None:
            slots[piece, k] = value
        elif count == 1:
            slots[piece, k, pl.ds(row, 1), :] = value
        else:
            slots[pl.ds(piece, count), k, row, :] = value

    return put


def chosen_margin(table, axis, message, work, before=None):
    for k in range(4):

        @pl.when(axis == k)
        def _(k=k):
            MARGINS[k](table, message_put(message), work, before)


def copy_slots(source, target):
    def body(piece, carry):
        for k in range(4):
            target[piece, k] = source[piece, k]
        return carry

    lax.fori_loop(0, PIECES, body, 0)


PREVIOUS, LAST, SOURCE, OWN_DROP, CHAIN_AXIS, CHAIN_SLOT, INFO = 0, 32, 160, 192, 192, 196, 256


def first_kernel(trees_in, potentials, message, info, hot, table, trees, *rest):
    work, load_sems, sems = rest[:4], rest[4], rest[5]
    me, s = lax.axis_index("clique"), lax.axis_index("subtree")
    size = 1024 // CHUNKS

    def load(n):
        at = pl.ds(pl.multiple_of(size * n, size), size)
        return pltpu.make_async_copy(potentials.at[at], table.at[at], load_sems.at[n])

    small = pltpu.make_async_copy(trees_in, trees, sems)
    small.start()
    for n in range(CHUNKS):
        load(n).start()
    prepare_place(hot)
    for n in range(128):
        info[LAST + n] = PIECES
    small.wait()
    info[PREVIOUS] = PIECES
    info[SOURCE] = trees[4 + s, 0]

    def link(c, carry):
        target = trees[8, c] * 4 + trees[4 + s, c]
        info[SOURCE + c] = target
        info[PREVIOUS + c] = info[LAST + target]
        info[LAST + target] = c
        return carry

    lax.fori_loop(1, PIECES, link, 0)
    own = trees[s, me]
    info[OWN_DROP] = own
    to_next = trees[4 + jnp.minimum(s + 1, 3), 0]
    to_previous = trees[s, 0]
    for step, sender, receiver in ((1, 0, 2), (2, 1, 1), (3, 2, 0)):
        active = (me == 0) & (((s == 1) | (s == 2)) == (step > 1))
        info[CHAIN_AXIS + step] = jnp.where(active, jnp.where(s == sender, to_next, to_previous), 4)
        info[CHAIN_SLOT + step] = jnp.where(s == receiver, to_next, to_previous)
    chosen_margin(table, own, message, work, lambda n: load(n).wait())


def up_kernel(info, hot, table, slots, message, placed, *work):
    place_slots(table, placed, slots, (work[4], hot))
    chosen_margin(placed, info[OWN_DROP], message, work)


def chain_first_kernel(info, hot, table, slots, message, placed, *work):
    place_slots(table, placed, slots, (work[4], hot))
    chosen_margin(placed, info[CHAIN_AXIS + 1], message, work)


def chain_kernel(step, info, hot, table, arrived, message, placed, *work):
    place_message(table, placed, arrived, info[CHAIN_SLOT + step - 1], (work[4], hot))
    chosen_margin(placed, info[CHAIN_AXIS + step], message, work)


def inner_root(s):
    return (s == 1) | (s == 2)


def last_root_slot(info):
    inner = inner_root(lax.axis_index("subtree"))
    return jnp.where(inner, info[CHAIN_SLOT + 1], info[CHAIN_SLOT + 3])


def final_kernel(info, hot, table, last_root, received, message, out, belief, held, left, sems):
    below = lax.axis_index("clique") != 0
    top = jnp.max(tree([received[piece] for piece in range(PIECES)], jnp.maximum))
    total = tree([jnp.exp(received[piece] - top) for piece in range(PIECES)], jnp.add)
    log_total = top + jnp.log(jnp.broadcast_to(jnp.sum(total), (8, 128)))
    for piece in range(PIECES):
        held[piece] = jnp.where(below, received[piece] - message[piece], last_root[piece]) - log_total

    def out_copy(part):
        at = pl.ds(pl.multiple_of(part * 256, 256), 256)
        return pltpu.make_async_copy(belief.at[at], out.at[at], sems.at[part])

    axis = jnp.where(below, info[OWN_DROP], last_root_slot(info))
    place_message(table, belief, held, axis, (left, hot), after=lambda part: out_copy(part).start())
    for part in range(4):
        out_copy(part).wait()


TURNS = sorted(
    (turn for turn in range(1, PIECES)),
    key=lambda turn: -(min(turn // 8, 4 - turn // 8) + min(turn // 2 % 4, 4 - turn // 2 % 4)),
)


def turned(me, turn):
    y, z, core = (me // 8 + turn // 8) % 4, (me // 2 % 4 + turn // 2 % 4) % 4, (me % 2 + turn % 2) % 2
    return y * 8 + z * 2 + core


def announce(me):
    barrier = pltpu.get_barrier_semaphore()
    for turn in TURNS:
        pl.semaphore_signal(barrier, inc=1, device_id={"clique": turned(me, turn)}, device_id_type=MESH)


def await_others():
    pl.semaphore_wait(pltpu.get_barrier_semaphore(), PIECES - 1)


def enter(me):
    announce(me)
    await_others()


def send_pieces(me, source, target, sems, prepare=None):
    for turn in TURNS:
        other = turned(me, turn)
        if prepare is not None:
            prepare(other)
        pltpu.make_async_remote_copy(
            src_ref=source.at[other],
            dst_ref=target.at[me],
            send_sem=sems.at[0],
            recv_sem=sems.at[1],
            device_id={"clique": other},
            device_id_type=MESH,
        ).start()


def part_of(me, count, source, target, sems):
    return pltpu.make_async_remote_copy(
        src_ref=source.at[pl.ds(0, count)],
        dst_ref=target.at[pl.ds(0, count)],
        send_sem=sems.at[0],
        recv_sem=sems.at[1],
        device_id={"clique": (me + 1) % PIECES},
        device_id_type=MESH,
    )


def all_but_one(me, source, target, sems):
    return part_of(me, PIECES - 1, source, target, sems)


def gather_up(me, info, message, arrived, sums, sems):
    enter(me)
    send_pieces(me, message, arrived, sems)
    arrived[me] = message[me]
    sums[PIECES] = jnp.zeros((8, 128), F32)
    all_but_one(me, message, arrived, sems).wait_recv()
    for c in range(1, PIECES):
        sums[c] = arrived[c] + sums[info[PREVIOUS + c]]
    all_but_one(me, message, arrived, sems).wait_send()


def sums_kernel(info, message, slots, arrived, sums, outgoing, sems, more_sems):
    me = lax.axis_index("clique")
    gather_up(me, info, message, arrived, sums, sems)

    def prepare(p):
        for k in range(4):
            outgoing[p, k] = sums[info[LAST + p * 4 + k]]

    send_pieces(me, outgoing, slots, more_sems, prepare)
    for k in range(4):
        slots[me, k] = sums[info[LAST + me * 4 + k]]
    all_but_one(me, outgoing, slots, more_sems).wait()


def root_sums_kernel(info, message, old_slots, slots, arrived, sums, outgoing, sems, more_sems):
    me = lax.axis_index("clique")
    gather_up(me, info, message, arrived, sums, sems)

    @pl.when(me != 0)
    def _():
        for k in range(4):
            outgoing[k] = sums[info[LAST + k]]
        copy = pltpu.make_async_remote_copy(
            src_ref=outgoing,
            dst_ref=slots.at[me],
            send_sem=more_sems.at[0],
            recv_sem=more_sems.at[1],
            device_id={"clique": 0},
            device_id_type=MESH,
        )
        copy.start()
        copy_slots(old_slots, slots)
        copy.wait_send()

    @pl.when(me == 0)
    def _():
        for k in range(4):
            slots[0, k] = sums[info[LAST + k]]
        all_but_one(me, slots, slots, more_sems).wait_recv()


def to_root(s, step, source, target, sems):
    partner = 3 - s if step == 2 else s + 1 - 2 * (s % 2)
    return partner, pltpu.make_async_remote_copy(
        src_ref=source,
        dst_ref=target,
        send_sem=sems.at[0],
        recv_sem=sems.at[1],
        device_id={"subtree": partner},
        device_id_type=MESH,
    )


def hop_kernel(step, sent, arrived, sems):
    me, s = lax.axis_index("clique"), lax.axis_index("subtree")
    partner, copy = to_root(s, step, sent, arrived, sems)
    barrier = pltpu.get_barrier_semaphore()
    receives = (me == 0) & inner_root(s)
    sends = (me == 0) & (inner_root(s) == (step == 2))

    @pl.when(receives)
    def _():
        pl.semaphore_signal(barrier, inc=1, device_id={"subtree": partner}, device_id_type=MESH)

    @pl.when(sends)
    def _():
        pl.semaphore_wait(barrier, 1)
        copy.start()

    @pl.when(jnp.logical_not(receives))
    def _():
        for piece in range(PIECES):
            arrived[piece] = jnp.zeros((8, 128), F32)

    @pl.when(receives)
    def _():
        copy.wait_recv()

    @pl.when(sends)
    def _():
        copy.wait_send()


def send_slots(me, start, source, target, sems):
    for turn in TURNS:
        other = turned(me, turn)
        pltpu.make_async_remote_copy(
            src_ref=source.at[other, pl.ds(start, 1)],
            dst_ref=target,
            send_sem=sems.at[0],
            recv_sem=sems.at[1],
            device_id={"clique": other},
            device_id_type=MESH,
        ).start()


def down_kernel(info, hot, table, first, sent, message, received, last_root, *scratch):
    belief, margins, held, arrived, from_root, third, out_1, in_1, out_2 = scratch[:9]
    work, sems = scratch[9:14], scratch[14:]
    tools = (work[4], hot)
    me, s = lax.axis_index("clique"), lax.axis_index("subtree")
    inner = inner_root(s)
    sends, receives = (me == 0) & inner, (me == 0) & jnp.logical_not(inner)
    partner, copy = to_root(s, 3, sent, third, sems[4])
    barrier = pltpu.get_barrier_semaphore()

    @pl.when(receives)
    def _():
        pl.semaphore_signal(barrier, inc=1, device_id={"subtree": partner}, device_id_type=MESH)

    announce(me)

    @pl.when(sends)
    def _():
        pl.semaphore_wait(barrier, PIECES)
        copy.start()

    @pl.when(jnp.logical_not(sends))
    def _():
        pl.semaphore_wait(barrier, PIECES - 1)

    def send_margins(pair, target, order):
        for group in order:
            if len(group) == 2:
                turned_margins(belief, slot_put(margins, 2), slot_put(margins, 3), work)
            else:
                MARGINS[group[0]](belief, slot_put(margins, group[0]), work)
            for k in group:
                send_slots(me, k, margins, target.at[pl.ds(k, 1)], pair)
        for k in range(4):
            target[k] = margins[me, k]

    @pl.when(receives)
    def _():
        copy.wait_recv()

        def body(piece, carry):
            last_root[piece] = third[piece]
            return carry

        lax.fori_loop(0, PIECES, body, 0, unroll=8)

    @pl.when(jnp.logical_not(receives))
    def _():
        def body(piece, carry):
            last_root[piece] = first[piece]
            return carry

        lax.fori_loop(0, PIECES, body, 0, unroll=8)

    @pl.when(me == 0)
    def _():
        slot = last_root_slot(info)

        def body(piece, carry):
            for k in range(4):
                held[piece, k] = jnp.where(slot == k, last_root[piece], 0.0)
            return carry

        lax.fori_loop(0, PIECES, body, 0, unroll=8)
        place_slots(table, belief, held, tools)
        send_margins(sems[0], from_root, ((2, 3), (1,), (0,)))

    @pl.when(me != 0)
    def _():
        pltpu.make_async_remote_copy(
            src_ref=from_root,
            dst_ref=from_root,
            send_sem=sems[0].at[0],
            recv_sem=sems[0].at[1],
            device_id={"clique": 0},
            device_id_type=MESH,
        ).wait_recv()

    for k in range(4):
        arrived[0, k] = from_root[k]

    def prepare_1(c):
        out_1[c] = from_root[info[SOURCE + c] % 4]

    send_pieces(me, out_1, in_1, sems[1], prepare_1)
    in_1[me] = from_root[info[SOURCE + me] % 4]
    all_but_one(me, out_1, in_1, sems[1]).wait()

    @pl.when(me != 0)
    def _():
        drop = info[OWN_DROP]

        def body(piece, carry):
            value = in_1[piece] - message[piece]
            for k in range(4):
                held[piece, k] = jnp.where(drop == k, value, 0.0)
            return carry

        lax.fori_loop(0, PIECES, body, 0, unroll=8)
        place_slots(table, belief, held, tools)
        send_margins(sems[2], arrived.at[me], ((0,), (1,), (2, 3)))
        part_of(me, PIECES - 2, margins, arrived, sems[2]).wait_recv()

    @pl.when(me == 0)
    def _():
        part_of(me, PIECES - 1, margins, arrived, sems[2]).wait_recv()

    def prepare_2(c):
        out_2[c] = arrived[info[SOURCE + c] // 4, info[SOURCE + c] % 4]

    send_pieces(me, out_2, received, sems[3], prepare_2)
    received[me] = arrived[info[SOURCE + me] // 4, info[SOURCE + me] % 4]
    all_but_one(me, out_2, received, sems[3]).wait()

    @pl.when(me == 0)
    def _():
        part_of(me, PIECES - 1, margins, arrived, sems[0]).wait_send()

    @pl.when(me != 0)
    def _():
        part_of(me, PIECES - 1, margins, arrived, sems[2]).wait_send()

    @pl.when(sends)
    def _():
        copy.wait_send()


MESSAGE = jax.ShapeDtypeStruct((PIECES, 8, 128), F32)
SLOTS = jax.ShapeDtypeStruct((PIECES, 4, 8, 128), F32)
TABLE = jax.ShapeDtypeStruct((1024, 1024), F32)
ANY_SPEC = pl.BlockSpec(memory_space=pl.ANY)
S_SPEC = pl.BlockSpec(memory_space=SMEM)
V_SPEC = pl.BlockSpec(memory_space=VMEM)
HELD_MESSAGE = VMEM((PIECES, 8, 128), F32)
HELD_SUMS = VMEM((PIECES + 1, 8, 128), F32)
HELD_SLOTS = VMEM((PIECES, 4, 8, 128), F32)
HELD_PIECE = VMEM((4, 8, 128), F32)
HELD_TABLE = VMEM((1024, 1024), F32)
LEFT = VMEM((256, 256), jnp.bfloat16)
HOT = jax.ShapeDtypeStruct((256, 1024), jnp.bfloat16)
WORK = [VMEM((1024, 128), F32), VMEM((8, 32, 128), F32), VMEM((8, 32, 128), F32), VMEM((8, 8, 128, 128), F32), LEFT]
PAIR_SEMS = pltpu.SemaphoreType.DMA((2,))


def call(kernel, name, ins, outs, out_specs, scratch, collective=None, limit=20):
    more = {} if collective is None else dict(collective_id=collective, has_side_effects=True)
    return pl.pallas_call(
        kernel,
        name=name,
        in_specs=ins,
        out_shape=outs,
        out_specs=out_specs,
        scratch_shapes=scratch,
        compiler_params=pltpu.CompilerParams(vmem_limit_bytes=limit * 2**20, **more),
    )


def per_device(potentials, parent, child_drop, parent_drop):
    table = potentials.reshape(1024, 1024)
    trees = jnp.concatenate([child_drop, parent_drop, parent])
    message, info, hot = call(
        first_kernel,
        "first",
        [ANY_SPEC] * 2,
        (MESSAGE, jax.ShapeDtypeStruct((INFO,), jnp.int32), HOT),
        (V_SPEC, S_SPEC, V_SPEC),
        [HELD_TABLE, SMEM((9, 32), jnp.int32)]
        + WORK[:4]
        + [pltpu.SemaphoreType.DMA((CHUNKS,)), pltpu.SemaphoreType.DMA],
        limit=53,
    )(trees, table)
    slots = call(
        sums_kernel,
        "sums",
        [S_SPEC, V_SPEC],
        SLOTS,
        V_SPEC,
        [HELD_MESSAGE, HELD_SUMS, HELD_SLOTS, PAIR_SEMS, PAIR_SEMS],
        collective=0,
    )(info, message)
    message = call(
        up_kernel, "up", [S_SPEC] + [V_SPEC] * 3, MESSAGE, V_SPEC, [HELD_TABLE] + WORK
    )(info, hot, table, slots)
    slots = call(
        root_sums_kernel,
        "root_sums",
        [S_SPEC] + [V_SPEC] * 2,
        SLOTS,
        V_SPEC,
        [HELD_MESSAGE, HELD_SUMS, HELD_PIECE, PAIR_SEMS, PAIR_SEMS],
        collective=1,
    )(info, message, slots)

    def hop(step, sent):
        return call(
            functools.partial(hop_kernel, step),
            f"hop_{step}",
            [V_SPEC],
            MESSAGE,
            V_SPEC,
            [PAIR_SEMS],
            collective=2 + step,
        )(sent)

    sent, table = call(
        chain_first_kernel, "chain_1", [S_SPEC] + [V_SPEC] * 3, (MESSAGE, TABLE), (V_SPEC, V_SPEC), WORK
    )(info, hot, table, slots)
    first = hop(1, sent)
    sent = call(
        functools.partial(chain_kernel, 2),
        "chain_2",
        [S_SPEC] + [V_SPEC] * 3,
        MESSAGE,
        V_SPEC,
        [HELD_TABLE] + WORK,
    )(info, hot, table, first)
    second = hop(2, sent)
    sent, table = call(
        functools.partial(chain_kernel, 3),
        "chain_3",
        [S_SPEC] + [V_SPEC] * 3,
        (MESSAGE, TABLE),
        (V_SPEC, V_SPEC),
        WORK,
    )(info, hot, table, second)
    received, last_root = call(
        down_kernel,
        "down",
        [S_SPEC] + [V_SPEC] * 5,
        (MESSAGE, MESSAGE),
        (V_SPEC, V_SPEC),
        [HELD_TABLE] + [HELD_SLOTS] * 3 + [HELD_PIECE] + [HELD_MESSAGE] * 4 + WORK + [PAIR_SEMS] * 5,
        collective=2,
    )(info, hot, table, first, sent, message)
    out = call(
        final_kernel,
        "final",
        [S_SPEC] + [V_SPEC] * 5,
        TABLE,
        ANY_SPEC,
        [HELD_TABLE, HELD_MESSAGE, LEFT, pltpu.SemaphoreType.DMA((4,))],
    )(info, hot, table, last_root, received, message)
    return out.reshape(1, 1, 1024, 1024)


def solution(mesh):
    specs = (P("subtree", "clique", None, None), P("subtree", None), P(), P())
    return jax.shard_map(
        per_device,
        mesh=mesh,
        in_specs=specs,
        out_specs=P("subtree", "clique", None, None),
        check_vma=False,
    )
```

```python
import functools

import jax
import jax.numpy as jnp
from jax import lax
from jax.experimental import pallas as pl
from jax.experimental.pallas import tpu as pltpu
from jax.sharding import PartitionSpec as P

PIECES = 32
CHUNKS = 8
MESH = pl.DeviceIdType.MESH
F32 = jnp.float32
VMEM = pltpu.VMEM
SMEM = pltpu.SMEM


def lanes():
    return lax.broadcasted_iota(jnp.int32, (8, 128), 1)


def rows():
    return lax.broadcasted_iota(jnp.int32, (8, 128), 0)


def take(vec, index):
    return jnp.take_along_axis(vec, index, axis=1, mode="promise_in_bounds")


def tree(parts, op):
    parts = list(parts)
    while len(parts) > 1:
        parts = [op(*parts[n : n + 2]) if n + 1 < len(parts) else parts[n] for n in range(0, len(parts), 2)]
    return parts[0]


def tile(table, a0, i, t):
    return table[pl.ds(pl.multiple_of(a0 * 32 + 8 * i, 8), 8), 128 * t : 128 * (t + 1)]


def prepare_place(hot):
    row = lax.broadcasted_iota(jnp.int32, (256, 1024), 0)
    column = lax.broadcasted_iota(jnp.int32, (256, 1024), 1)
    level = jnp.where(row < 128, column // 32, column % 32)
    hot[...] = jnp.where((level == row % 32) & (row % 128 < 96), 1.0, 0.0).astype(jnp.bfloat16)


def three_parts(vec):
    high = vec.astype(jnp.bfloat16).astype(F32)
    rest = vec - high
    middle = rest.astype(jnp.bfloat16).astype(F32)
    group = lanes() // 32
    return jnp.where(group == 0, high, jnp.where(group == 1, middle, jnp.where(group == 2, rest - middle, 0.0)))


def place(source, target, terms, tools, after=None):
    left, hot = tools
    lane, row = lanes(), rows()
    spread = (row % 4) * 32 + lane % 32
    by_matrix = [k for k in (3, 2) if k in terms] if 3 in terms else []
    depth = 128 * len(by_matrix)

    def body(part, carry):
        def levels(k, s, i):
            read = terms[k][1]
            return take(jnp.where(row < 4, read(part * 8 + 2 * i, s), read(part * 8 + 2 * i + 1, s)), spread)

        if by_matrix:
            for s in range(8):
                for half in range(2):
                    both = [
                        jnp.concatenate([three_parts(levels(k, s, i)) for k in by_matrix], axis=1)
                        for i in (2 * half, 2 * half + 1)
                    ]
                    at = 32 * s + 16 * half
                    left[at : at + 16, :depth] = jnp.concatenate(both, axis=0).astype(jnp.bfloat16)
        for n in range(4):
            if by_matrix:
                back = jnp.dot(
                    left[:, :depth], hot[:depth, 256 * n : 256 * (n + 1)], preferred_element_type=F32
                )
            for s in range(8):
                a0 = part * 8 + s
                third = [levels(2, s, i) for i in range(4)] if 2 in terms and not by_matrix else None
                for t in (2 * n, 2 * n + 1):
                    second = terms[1][1](part * 8 + t, s) if 1 in terms else None
                    for i in range(4):
                        adds = []
                        if 0 in terms:
                            adds.append(terms[0][0](i * 8 + t))
                        if 1 in terms:
                            adds.append(jnp.broadcast_to(second, (8, 128)))
                        if third is not None:
                            adds.append(third[i])
                        if by_matrix:
                            at, column = 32 * s + 8 * i, 128 * (t - 2 * n)
                            adds.append(back[at : at + 8, column : column + 128])
                        where = pl.ds(pl.multiple_of(a0 * 32 + 8 * i, 8), 8)
                        value = tile(source, a0, i, t) + functools.reduce(jnp.add, adds)
                        target[where, 128 * t : 128 * (t + 1)] = value
        if after is not None:
            after(part)
        return carry

    lax.fori_loop(0, 4, body, 0)


def place_slots(source, target, slots, tools, after=None):
    def readers(k):
        return lambda piece: slots[piece, k], lambda piece, s: slots[piece, k, pl.ds(s, 1), :]

    place(source, target, {k: readers(k) for k in range(4)}, tools, after)


def place_message(source, target, message, axis, tools, after=None):
    for k in range(4):

        @pl.when(axis == k)
        def _(k=k):
            readers = (lambda piece: message[piece], lambda piece, s: message[piece, pl.ds(s, 1), :])
            place(source, target, {k: readers}, tools, after)


def pick(parts):
    group = lanes() // 32
    return jnp.where(
        group == 0, parts[0], jnp.where(group == 1, parts[1], jnp.where(group == 2, parts[2], parts[3]))
    )


def margin_0(table, put, work, before=None):
    if before is not None:
        for n in range(CHUNKS):
            before(n)

    def body(i, carry):
        for t in range(8):
            parts = [tile(table, a0, i, t) for a0 in range(32)]
            top = tree(parts, jnp.maximum)
            total = tree([jnp.exp(part - top) for part in parts], jnp.add)
            put(i * 8 + t, 1, None, top + jnp.log(total))
        return carry

    lax.fori_loop(0, 4, body, 0)


def over_rows(vec, op):
    for shift in (4, 2, 1):
        vec = op(vec, pltpu.roll(vec, shift, 0))
    return vec


def by_blocks(body, before):
    def block(n, carry):
        if before is not None:
            before(n)
        for a0 in range(4):
            body(n * 4 + a0, carry)
        return carry

    lax.fori_loop(0, 8, block, 0)


def margin_1(table, put, work, before=None):
    def body(a0, carry):
        for t in range(8):
            parts = [tile(table, a0, i, t) for i in range(4)]
            top = over_rows(tree(parts, jnp.maximum), jnp.maximum)
            total = over_rows(tree([jnp.exp(part - top) for part in parts], jnp.add), jnp.add)
            put((a0 // 8) * 8 + t, 1, a0 % 8, (top + jnp.log(total))[0:1])
        return carry

    by_blocks(body, before)


def put_turned(across, flat, put):
    for block in range(8):
        part = across[block]
        flat[128 * block : 128 * (block + 1), :] = jnp.concatenate([part] * 4, axis=0).T
    for a0 in range(32):
        put((a0 // 8) * 8, 8, a0 % 8, pick([flat[pl.ds(a0 * 32 + q, 8, stride=4), :] for q in range(4)]))


def turned_margins(table, put_2, put_3, work, before=None):
    flat, across_2, across_3, kept = work[:4]

    def body(block, carry):
        if before is not None:
            before(block)
        tops = None
        for t in range(8):
            turned = table[pl.ds(pl.multiple_of(block * 128, 128), 128), 128 * t : 128 * (t + 1)].T
            tiles = [[turned[32 * g + 8 * m : 32 * g + 8 * (m + 1)] for m in range(4)] for g in range(4)]
            if put_3 is not None:
                for g in range(4):
                    top = over_rows(tree(tiles[g], jnp.maximum), jnp.maximum)
                    total = over_rows(tree([jnp.exp(part - top) for part in tiles[g]], jnp.add), jnp.add)
                    across_3[block, 4 * t + g : 4 * t + g + 1, :] = (top + jnp.log(total))[0:1]
            if put_2 is not None:
                kept[block, t] = turned
                here = [tree([tiles[g][m] for g in range(4)], jnp.maximum) for m in range(4)]
                tops = here if tops is None else [jnp.maximum(a, b) for a, b in zip(tops, here)]
        if put_2 is not None:
            totals = None
            for t in range(8):
                here = [
                    tree(
                        [jnp.exp(kept[block, t, 32 * g + 8 * m : 32 * g + 8 * (m + 1), :] - tops[m]) for g in range(4)],
                        jnp.add,
                    )
                    for m in range(4)
                ]
                totals = here if totals is None else [a + b for a, b in zip(totals, here)]
            for m in range(4):
                across_2[block, 8 * m : 8 * (m + 1), :] = tops[m] + jnp.log(totals[m])
        return carry

    lax.fori_loop(0, 8, body, 0, unroll=4 if put_2 and put_3 else 8)
    if put_2 is not None:
        put_turned(across_2, flat, put_2)
    if put_3 is not None:
        put_turned(across_3, flat, put_3)


def margin_2(table, put, work, before=None):
    turned_margins(table, put, None, work, before)


def margin_3(table, put, work, before=None):
    turned_margins(table, None, put, work, before)


MARGINS = (margin_0, margin_1, margin_2, margin_3)


def message_put(message):
    def put(piece, count, row, value):
        if row is None:
            message[piece] = value
        elif count == 1:
            message[piece, pl.ds(row, 1), :] = value
        else:
            message[pl.ds(piece, count), row, :] = value

    return put


def slot_put(slots, k):
    def put(piece, count, row, value):
        if row is None:
            slots[piece, k] = value
        elif count == 1:
            slots[piece, k, pl.ds(row, 1), :] = value
        else:
            slots[pl.ds(piece, count), k, row, :] = value

    return put


def chosen_margin(table, axis, message, work, before=None):
    for k in range(4):

        @pl.when(axis == k)
        def _(k=k):
            MARGINS[k](table, message_put(message), work, before)


def copy_slots(source, target):
    def body(piece, carry):
        for k in range(4):
            target[piece, k] = source[piece, k]
        return carry

    lax.fori_loop(0, PIECES, body, 0)


PREVIOUS, LAST, SOURCE, OWN_DROP, CHAIN_AXIS, CHAIN_SLOT, INFO = 0, 32, 160, 192, 192, 196, 256


def first_kernel(trees_in, potentials, message, info, hot, table, trees, *rest):
    work, load_sems, sems = rest[:4], rest[4], rest[5]
    me, s = lax.axis_index("clique"), lax.axis_index("subtree")
    size = 1024 // CHUNKS

    def load(n):
        at = pl.ds(pl.multiple_of(size * n, size), size)
        return pltpu.make_async_copy(potentials.at[at], table.at[at], load_sems.at[n])

    small = pltpu.make_async_copy(trees_in, trees, sems)
    small.start()
    for n in range(CHUNKS):
        load(n).start()
    prepare_place(hot)
    for n in range(128):
        info[LAST + n] = PIECES
    small.wait()
    info[PREVIOUS] = PIECES
    info[SOURCE] = trees[4 + s, 0]

    def link(c, carry):
        target = trees[8, c] * 4 + trees[4 + s, c]
        info[SOURCE + c] = target
        info[PREVIOUS + c] = info[LAST + target]
        info[LAST + target] = c
        return carry

    lax.fori_loop(1, PIECES, link, 0)
    own = trees[s, me]
    info[OWN_DROP] = own
    to_next = trees[4 + jnp.minimum(s + 1, 3), 0]
    to_previous = trees[s, 0]
    for step, sender, receiver in ((1, 0, 2), (2, 1, 1), (3, 2, 0)):
        active = (me == 0) & (((s == 1) | (s == 2)) == (step > 1))
        info[CHAIN_AXIS + step] = jnp.where(active, jnp.where(s == sender, to_next, to_previous), 4)
        info[CHAIN_SLOT + step] = jnp.where(s == receiver, to_next, to_previous)
    chosen_margin(table, own, message, work, lambda n: load(n).wait())


def up_kernel(info, hot, table, slots, message, placed, *work):
    place_slots(table, placed, slots, (work[4], hot))
    chosen_margin(placed, info[OWN_DROP], message, work)


def chain_first_kernel(info, hot, table, slots, message, placed, *work):
    place_slots(table, placed, slots, (work[4], hot))
    chosen_margin(placed, info[CHAIN_AXIS + 1], message, work)


def chain_kernel(step, info, hot, table, arrived, message, placed, *work):
    place_message(table, placed, arrived, info[CHAIN_SLOT + step - 1], (work[4], hot))
    chosen_margin(placed, info[CHAIN_AXIS + step], message, work)


def inner_root(s):
    return (s == 1) | (s == 2)


def last_root_slot(info):
    inner = inner_root(lax.axis_index("subtree"))
    return jnp.where(inner, info[CHAIN_SLOT + 1], info[CHAIN_SLOT + 3])


def final_kernel(info, hot, table, last_root, received, message, out, belief, held, left, sems):
    below = lax.axis_index("clique") != 0
    top = jnp.max(tree([received[piece] for piece in range(PIECES)], jnp.maximum))
    total = tree([jnp.exp(received[piece] - top) for piece in range(PIECES)], jnp.add)
    log_total = top + jnp.log(jnp.broadcast_to(jnp.sum(total), (8, 128)))
    for piece in range(PIECES):
        held[piece] = jnp.where(below, received[piece] - message[piece], last_root[piece]) - log_total

    def out_copy(part):
        at = pl.ds(pl.multiple_of(part * 256, 256), 256)
        return pltpu.make_async_copy(belief.at[at], out.at[at], sems.at[part])

    axis = jnp.where(below, info[OWN_DROP], last_root_slot(info))
    place_message(table, belief, held, axis, (left, hot), after=lambda part: out_copy(part).start())
    for part in range(4):
        out_copy(part).wait()


TURNS = sorted(
    (turn for turn in range(1, PIECES)),
    key=lambda turn: -(min(turn // 8, 4 - turn // 8) + min(turn // 2 % 4, 4 - turn // 2 % 4)),
)


def turned(me, turn):
    y, z, core = (me // 8 + turn // 8) % 4, (me // 2 % 4 + turn // 2 % 4) % 4, (me % 2 + turn % 2) % 2
    return y * 8 + z * 2 + core


def announce(me):
    barrier = pltpu.get_barrier_semaphore()
    for turn in TURNS:
        pl.semaphore_signal(barrier, inc=1, device_id={"clique": turned(me, turn)}, device_id_type=MESH)


def await_others():
    pl.semaphore_wait(pltpu.get_barrier_semaphore(), PIECES - 1)


def enter(me):
    announce(me)
    await_others()


def send_pieces(me, source, target, sems, prepare=None):
    for turn in TURNS:
        other = turned(me, turn)
        if prepare is not None:
            prepare(other)
        pltpu.make_async_remote_copy(
            src_ref=source.at[other],
            dst_ref=target.at[me],
            send_sem=sems.at[0],
            recv_sem=sems.at[1],
            device_id={"clique": other},
            device_id_type=MESH,
        ).start()


def part_of(me, count, source, target, sems):
    return pltpu.make_async_remote_copy(
        src_ref=source.at[pl.ds(0, count)],
        dst_ref=target.at[pl.ds(0, count)],
        send_sem=sems.at[0],
        recv_sem=sems.at[1],
        device_id={"clique": (me + 1) % PIECES},
        device_id_type=MESH,
    )


def all_but_one(me, source, target, sems):
    return part_of(me, PIECES - 1, source, target, sems)


def gather_up(me, info, message, arrived, sums, sems):
    enter(me)
    send_pieces(me, message, arrived, sems)
    arrived[me] = message[me]
    sums[PIECES] = jnp.zeros((8, 128), F32)
    all_but_one(me, message, arrived, sems).wait_recv()
    for c in range(1, PIECES):
        sums[c] = arrived[c] + sums[info[PREVIOUS + c]]
    all_but_one(me, message, arrived, sems).wait_send()


def sums_kernel(info, message, slots, arrived, sums, outgoing, sems, more_sems):
    me = lax.axis_index("clique")
    gather_up(me, info, message, arrived, sums, sems)

    def prepare(p):
        for k in range(4):
            outgoing[p, k] = sums[info[LAST + p * 4 + k]]

    send_pieces(me, outgoing, slots, more_sems, prepare)
    for k in range(4):
        slots[me, k] = sums[info[LAST + me * 4 + k]]
    all_but_one(me, outgoing, slots, more_sems).wait()


def root_sums_kernel(info, message, old_slots, slots, arrived, sums, outgoing, sems, more_sems):
    me = lax.axis_index("clique")
    gather_up(me, info, message, arrived, sums, sems)

    @pl.when(me != 0)
    def _():
        for k in range(4):
            outgoing[k] = sums[info[LAST + k]]
        copy = pltpu.make_async_remote_copy(
            src_ref=outgoing,
            dst_ref=slots.at[me],
            send_sem=more_sems.at[0],
            recv_sem=more_sems.at[1],
            device_id={"clique": 0},
            device_id_type=MESH,
        )
        copy.start()
        copy_slots(old_slots, slots)
        copy.wait_send()

    @pl.when(me == 0)
    def _():
        for k in range(4):
            slots[0, k] = sums[info[LAST + k]]
        all_but_one(me, slots, slots, more_sems).wait_recv()


def to_root(s, step, source, target, sems):
    partner = 3 - s if step == 2 else s + 1 - 2 * (s % 2)
    return partner, pltpu.make_async_remote_copy(
        src_ref=source,
        dst_ref=target,
        send_sem=sems.at[0],
        recv_sem=sems.at[1],
        device_id={"subtree": partner},
        device_id_type=MESH,
    )


def hop_kernel(step, sent, arrived, sems):
    me, s = lax.axis_index("clique"), lax.axis_index("subtree")
    partner, copy = to_root(s, step, sent, arrived, sems)
    barrier = pltpu.get_barrier_semaphore()
    receives = (me == 0) & inner_root(s)
    sends = (me == 0) & (inner_root(s) == (step == 2))

    @pl.when(receives)
    def _():
        pl.semaphore_signal(barrier, inc=1, device_id={"subtree": partner}, device_id_type=MESH)

    @pl.when(sends)
    def _():
        pl.semaphore_wait(barrier, 1)
        copy.start()

    @pl.when(jnp.logical_not(receives))
    def _():
        for piece in range(PIECES):
            arrived[piece] = jnp.zeros((8, 128), F32)

    @pl.when(receives)
    def _():
        copy.wait_recv()

    @pl.when(sends)
    def _():
        copy.wait_send()


def send_slots(me, start, source, target, sems):
    for turn in TURNS:
        other = turned(me, turn)
        pltpu.make_async_remote_copy(
            src_ref=source.at[other, pl.ds(start, 1)],
            dst_ref=target,
            send_sem=sems.at[0],
            recv_sem=sems.at[1],
            device_id={"clique": other},
            device_id_type=MESH,
        ).start()


def down_kernel(info, hot, table, first, sent, message, received, last_root, *scratch):
    belief, margins, held, arrived, from_root, third, out_1, in_1, out_2 = scratch[:9]
    work, sems = scratch[9:14], scratch[14:]
    tools = (work[4], hot)
    me, s = lax.axis_index("clique"), lax.axis_index("subtree")
    inner = inner_root(s)
    sends, receives = (me == 0) & inner, (me == 0) & jnp.logical_not(inner)
    partner, copy = to_root(s, 3, sent, third, sems[4])
    barrier = pltpu.get_barrier_semaphore()

    @pl.when(receives)
    def _():
        pl.semaphore_signal(barrier, inc=1, device_id={"subtree": partner}, device_id_type=MESH)

    announce(me)

    @pl.when(sends)
    def _():
        pl.semaphore_wait(barrier, PIECES)
        copy.start()

    @pl.when(jnp.logical_not(sends))
    def _():
        pl.semaphore_wait(barrier, PIECES - 1)

    def send_margins(pair, target, order):
        for group in order:
            if len(group) == 2:
                turned_margins(belief, slot_put(margins, 2), slot_put(margins, 3), work)
            else:
                MARGINS[group[0]](belief, slot_put(margins, group[0]), work)
            for k in group:
                send_slots(me, k, margins, target.at[pl.ds(k, 1)], pair)
        for k in range(4):
            target[k] = margins[me, k]

    @pl.when(receives)
    def _():
        copy.wait_recv()

        def body(piece, carry):
            last_root[piece] = third[piece]
            return carry

        lax.fori_loop(0, PIECES, body, 0, unroll=8)

    @pl.when(jnp.logical_not(receives))
    def _():
        def body(piece, carry):
            last_root[piece] = first[piece]
            return carry

        lax.fori_loop(0, PIECES, body, 0, unroll=8)

    @pl.when(me == 0)
    def _():
        slot = last_root_slot(info)

        def body(piece, carry):
            for k in range(4):
                held[piece, k] = jnp.where(slot == k, last_root[piece], 0.0)
            return carry

        lax.fori_loop(0, PIECES, body, 0, unroll=8)
        place_slots(table, belief, held, tools)
        send_margins(sems[0], from_root, ((2, 3), (1,), (0,)))

    @pl.when(me != 0)
    def _():
        pltpu.make_async_remote_copy(
            src_ref=from_root,
            dst_ref=from_root,
            send_sem=sems[0].at[0],
            recv_sem=sems[0].at[1],
            device_id={"clique": 0},
            device_id_type=MESH,
        ).wait_recv()

    for k in range(4):
        arrived[0, k] = from_root[k]

    def prepare_1(c):
        out_1[c] = from_root[info[SOURCE + c] % 4]

    send_pieces(me, out_1, in_1, sems[1], prepare_1)
    in_1[me] = from_root[info[SOURCE + me] % 4]
    all_but_one(me, out_1, in_1, sems[1]).wait()

    @pl.when(me != 0)
    def _():
        drop = info[OWN_DROP]

        def body(piece, carry):
            value = in_1[piece] - message[piece]
            for k in range(4):
                held[piece, k] = jnp.where(drop == k, value, 0.0)
            return carry

        lax.fori_loop(0, PIECES, body, 0, unroll=8)
        place_slots(table, belief, held, tools)
        send_margins(sems[2], arrived.at[me], ((0,), (1,), (2, 3)))
        part_of(me, PIECES - 2, margins, arrived, sems[2]).wait_recv()

    @pl.when(me == 0)
    def _():
        part_of(me, PIECES - 1, margins, arrived, sems[2]).wait_recv()

    def prepare_2(c):
        out_2[c] = arrived[info[SOURCE + c] // 4, info[SOURCE + c] % 4]

    send_pieces(me, out_2, received, sems[3], prepare_2)
    received[me] = arrived[info[SOURCE + me] // 4, info[SOURCE + me] % 4]
    all_but_one(me, out_2, received, sems[3]).wait()

    @pl.when(me == 0)
    def _():
        part_of(me, PIECES - 1, margins, arrived, sems[0]).wait_send()

    @pl.when(me != 0)
    def _():
        part_of(me, PIECES - 1, margins, arrived, sems[2]).wait_send()

    @pl.when(sends)
    def _():
        copy.wait_send()


MESSAGE = jax.ShapeDtypeStruct((PIECES, 8, 128), F32)
SLOTS = jax.ShapeDtypeStruct((PIECES, 4, 8, 128), F32)
TABLE = jax.ShapeDtypeStruct((1024, 1024), F32)
ANY_SPEC = pl.BlockSpec(memory_space=pl.ANY)
S_SPEC = pl.BlockSpec(memory_space=SMEM)
V_SPEC = pl.BlockSpec(memory_space=VMEM)
HELD_MESSAGE = VMEM((PIECES, 8, 128), F32)
HELD_SUMS = VMEM((PIECES + 1, 8, 128), F32)
HELD_SLOTS = VMEM((PIECES, 4, 8, 128), F32)
HELD_PIECE = VMEM((4, 8, 128), F32)
HELD_TABLE = VMEM((1024, 1024), F32)
LEFT = VMEM((256, 256), jnp.bfloat16)
HOT = jax.ShapeDtypeStruct((256, 1024), jnp.bfloat16)
WORK = [VMEM((1024, 128), F32), VMEM((8, 32, 128), F32), VMEM((8, 32, 128), F32), VMEM((8, 8, 128, 128), F32), LEFT]
PAIR_SEMS = pltpu.SemaphoreType.DMA((2,))


def call(kernel, name, ins, outs, out_specs, scratch, collective=None, limit=20):
    more = {} if collective is None else dict(collective_id=collective, has_side_effects=True)
    return pl.pallas_call(
        kernel,
        name=name,
        in_specs=ins,
        out_shape=outs,
        out_specs=out_specs,
        scratch_shapes=scratch,
        compiler_params=pltpu.CompilerParams(vmem_limit_bytes=limit * 2**20, **more),
    )


def per_device(potentials, parent, child_drop, parent_drop):
    table = potentials.reshape(1024, 1024)
    trees = jnp.concatenate([child_drop, parent_drop, parent])
    message, info, hot = call(
        first_kernel,
        "first",
        [ANY_SPEC] * 2,
        (MESSAGE, jax.ShapeDtypeStruct((INFO,), jnp.int32), HOT),
        (V_SPEC, S_SPEC, V_SPEC),
        [HELD_TABLE, SMEM((9, 32), jnp.int32)]
        + WORK[:4]
        + [pltpu.SemaphoreType.DMA((CHUNKS,)), pltpu.SemaphoreType.DMA],
        limit=53,
    )(trees, table)
    slots = call(
        sums_kernel,
        "sums",
        [S_SPEC, V_SPEC],
        SLOTS,
        V_SPEC,
        [HELD_MESSAGE, HELD_SUMS, HELD_SLOTS, PAIR_SEMS, PAIR_SEMS],
        collective=0,
    )(info, message)
    message = call(
        up_kernel, "up", [S_SPEC] + [V_SPEC] * 3, MESSAGE, V_SPEC, [HELD_TABLE] + WORK
    )(info, hot, table, slots)
    slots = call(
        root_sums_kernel,
        "root_sums",
        [S_SPEC] + [V_SPEC] * 2,
        SLOTS,
        V_SPEC,
        [HELD_MESSAGE, HELD_SUMS, HELD_PIECE, PAIR_SEMS, PAIR_SEMS],
        collective=1,
    )(info, message, slots)

    def hop(step, sent):
        return call(
            functools.partial(hop_kernel, step),
            f"hop_{step}",
            [V_SPEC],
            MESSAGE,
            V_SPEC,
            [PAIR_SEMS],
            collective=2 + step,
        )(sent)

    sent, table = call(
        chain_first_kernel, "chain_1", [S_SPEC] + [V_SPEC] * 3, (MESSAGE, TABLE), (V_SPEC, V_SPEC), WORK
    )(info, hot, table, slots)
    first = hop(1, sent)
    sent = call(
        functools.partial(chain_kernel, 2),
        "chain_2",
        [S_SPEC] + [V_SPEC] * 3,
        MESSAGE,
        V_SPEC,
        [HELD_TABLE] + WORK,
    )(info, hot, table, first)
    second = hop(2, sent)
    sent, table = call(
        functools.partial(chain_kernel, 3),
        "chain_3",
        [S_SPEC] + [V_SPEC] * 3,
        (MESSAGE, TABLE),
        (V_SPEC, V_SPEC),
        WORK,
    )(info, hot, table, second)
    received, last_root = call(
        down_kernel,
        "down",
        [S_SPEC] + [V_SPEC] * 5,
        (MESSAGE, MESSAGE),
        (V_SPEC, V_SPEC),
        [HELD_TABLE] + [HELD_SLOTS] * 3 + [HELD_PIECE] + [HELD_MESSAGE] * 4 + WORK + [PAIR_SEMS] * 5,
        collective=2,
    )(info, hot, table, first, sent, message)
    out = call(
        final_kernel,
        "final",
        [S_SPEC] + [V_SPEC] * 5,
        TABLE,
        ANY_SPEC,
        [HELD_TABLE, HELD_MESSAGE, LEFT, pltpu.SemaphoreType.DMA((4,))],
    )(info, hot, table, last_root, received, message)
    return out.reshape(1, 1, 1024, 1024)


def solution(mesh):
    specs = (P("subtree", "clique", None, None), P("subtree", None), P(), P())
    return jax.shard_map(
        per_device,
        mesh=mesh,
        in_specs=specs,
        out_specs=P("subtree", "clique", None, None),
        check_vma=False,
    )
```
